128 devices in a mesh: dp: 4 (over x_hi, core), fsdp: 32 (over y, z, x_lo).
Axes of the slice: x: 4 (x_hi: 2, x_lo: 2; x = x_hi * 2 + x_lo), y: 4, z: 4, core: 2. Of those that a mesh axis runs over, the one named last changes fastest.
Arguments:
- tokens: bfloat16 [16384, 1024], P(('dp', 'fsdp')), may hold values from -6 to 6
- lengths: int32 [128], P(('dp', 'fsdp')), may hold values from 1 to 128, as said below
- attn_gain: bfloat16 [1024], P(('dp', 'fsdp')), may hold values from 0.5 to 1.5
- w_qkv: bfloat16 [1024, 3072], P(('dp', 'fsdp')), may hold values from -0.1875 to 0.1875
- w_lr: bfloat16 [1024, 16], P(('dp', 'fsdp')), may hold values from -0.1875 to 0.1875
- init_w: bfloat16 [1024, 64], P(('dp', 'fsdp')), may hold values from -0.75 to 0.75
- init_b: bfloat16 [1024], P(('dp', 'fsdp')), may hold values from -3 to 3
- inner_gain: bfloat16 [1024], P(('dp', 'fsdp')), may hold values from 0.5 to 1.5
- inner_bias: bfloat16 [1024], P(('dp', 'fsdp')), may hold values from -2 to 2
- post_gain: bfloat16 [1024], P(('dp', 'fsdp')), may hold values from 0.5 to 1.5
- w_out: bfloat16 [1024, 1024], P(('dp', 'fsdp')), may hold values from -0.1875 to 0.1875
- ffn_gain: bfloat16 [1024], P(('dp', 'fsdp')), may hold values from 0.5 to 1.5
- w_gate: bfloat16 [1024, 2736], P(('dp', 'fsdp')), may hold values from -0.1875 to 0.1875
- w_up: bfloat16 [1024, 2736], P(('dp', 'fsdp')), may hold values from -0.1875 to 0.1875
- w_down: bfloat16 [2736, 1024], P(None, ('dp', 'fsdp')), may hold values from -0.109375 to 0.109375
- d_out: bfloat16 [16384, 1024], P(('dp', 'fsdp')), may hold values from -6 to 6
Outputs:
- output: bfloat16 [16384, 1024], P(('dp', 'fsdp'))
- d_tokens: float32 [16384, 1024], P(('dp', 'fsdp'))
- g_attn_gain: float32 [1024], P(('dp', 'fsdp'))
- g_w_qkv: float32 [1024, 3072], P(('dp', 'fsdp'))
- g_w_lr: float32 [1024, 16], P(('dp', 'fsdp'))
- g_init_w: float32 [1024, 64], P(('dp', 'fsdp'))
- g_init_b: float32 [1024], P(('dp', 'fsdp'))
- g_inner_gain: float32 [1024], P(('dp', 'fsdp'))
- g_inner_bias: float32 [1024], P(('dp', 'fsdp'))
- g_post_gain: float32 [1024], P(('dp', 'fsdp'))
- g_w_out: float32 [1024, 1024], P(('dp', 'fsdp'))
- g_ffn_gain: float32 [1024], P(('dp', 'fsdp'))
- g_w_gate: float32 [1024, 2736], P(('dp', 'fsdp'))
- g_w_up: float32 [1024, 2736], P(('dp', 'fsdp'))
- g_w_down: float32 [2736, 1024], P(None, ('dp', 'fsdp'))
The draws below stay inside these ranges and needn't reach their ends.
Inputs may be any that keep to these rules, and one draw needn't show every extreme that they name: `lengths`: some sequence has all 128 tokens valid.
All inputs are finite; a program needn't handle non-finite values.
Results may differ from the reference program's by a relative error of at most 0.0095.
Values may be sent and summed in bfloat16 or wider, within the bound.
A program may use at most 320 MiB of HBM per device.

```python
import math
import jax
import jax.numpy as jnp
from jax import lax

D = 1024
HEADS = 16
HEAD_DIM = 64
FF = 2736
MINI = 16
TOK_DEV = 128
SEQS = 128
TOKENS = 16384


def draw_lengths(key, part):
    key = jax.random.fold_in(key, 7)
    first, second = jax.random.split(key)
    values = jax.random.randint(first, (SEQS,), 1, TOK_DEV + 1)
    chosen = jax.random.randint(second, (), 0, SEQS)
    return jnp.where(jnp.arange(SEQS) == chosen, TOK_DEV, values).astype(jnp.int32)


def block_scale(key, extent, cuts, low, high):
    def one(axis_at, blocks):
        steps = jax.random.uniform(jax.random.fold_in(jax.random.fold_in(key, 6), axis_at), (blocks,), jnp.float32, low / len(cuts), high / len(cuts))
        return jnp.repeat(jnp.exp(steps), extent[axis_at] // blocks).reshape((-1,) + (1,) * (len(extent) - axis_at - 1))

    gain = one(*cuts[0])
    for cut in cuts[1:]:
        gain = gain * one(*cut)
    return gain


def centred(stream_key, extent, scale, reach, cuts=(), kind=jnp.bfloat16):
    values = scale * jax.random.normal(stream_key, extent, jnp.float32)
    if cuts:
        values = values * block_scale(stream_key, extent, cuts, -0.22, 0.18)
    return jnp.clip(values, -reach, reach).astype(kind)


def setup_inputs(seed: int = 0) -> dict:
    splits = jax.random.split(jax.random.key(seed), 17)
    return {
        "tokens": centred(splits[0], (TOKENS, D), 1.0, 6.0, ((0, 128),)),
        "lengths": draw_lengths(jax.random.fold_in(splits[16], 71), 0),
        "attn_gain": jnp.clip(1.0 + 0.1 * jax.random.normal(splits[2], (D,), jnp.float32), 0.5, 1.5).astype(jnp.bfloat16),
        "w_qkv": centred(splits[3], (D, 3 * D), D ** -0.5, 0.1875, ((0, 128),)),
        "w_lr": centred(splits[4], (D, HEADS), D ** -0.5, 0.1875, ((0, 128),)),
        "init_w": centred(splits[5], (D, HEAD_DIM), HEAD_DIM ** -0.5, 0.75, ((0, 128),)),
        "init_b": centred(splits[6], (D,), 0.5, 3.0, ((0, 128),)),
        "inner_gain": jnp.clip(1.0 + 0.1 * jax.random.normal(splits[7], (D,), jnp.float32), 0.5, 1.5).astype(jnp.bfloat16),
        "inner_bias": centred(splits[8], (D,), 0.3, 2.0, ((0, 128),)),
        "post_gain": jnp.clip(1.0 + 0.1 * jax.random.normal(splits[9], (D,), jnp.float32), 0.5, 1.5).astype(jnp.bfloat16),
        "w_out": centred(splits[10], (D, D), D ** -0.5, 0.1875, ((0, 128),)),
        "ffn_gain": jnp.clip(1.0 + 0.1 * jax.random.normal(splits[11], (D,), jnp.float32), 0.5, 1.5).astype(jnp.bfloat16),
        "w_gate": centred(splits[12], (D, FF), D ** -0.5, 0.1875, ((0, 128),)),
        "w_up": centred(splits[13], (D, FF), D ** -0.5, 0.1875, ((0, 128),)),
        "w_down": centred(splits[14], (FF, D), FF ** -0.5, 0.109375, ((1, 128),)),
        "d_out": centred(splits[15], (TOKENS, D), 1.0, 6.0, ((0, 128),)),
    }


HIGH = lax.Precision.HIGHEST
epsilon = 1e-06
inner_rate = 1.0

@jax.custom_vjp
def low(v):
    return lax.optimization_barrier(v.astype(jnp.bfloat16)).astype(jnp.float32)

@jax.custom_vjp
def low_back(v):
    return v

def low_keep(v):
    return (low(v), None)

def low_pass(kept, grad):
    return (grad,)

def back_keep(v):
    return (v, None)

def back_low(kept, grad):
    return (low(grad),)
low.defvjp(low_keep, low_pass)
low_back.defvjp(back_keep, back_low)

def rms_scale(values):
    return values * lax.rsqrt(lax.optimization_barrier(jnp.mean(values * values, -1, keepdims=True)) + epsilon)

def center_scale(values):
    center = values - lax.optimization_barrier(jnp.mean(values, -1, keepdims=True))
    return center * lax.rsqrt(lax.optimization_barrier(jnp.mean(center * center, -1, keepdims=True)) + epsilon)

def inner_step(state, item, gamma, beta):
    weight, bias = state
    query, keys, values, rate, keep = item
    size = keys.shape[1]
    hidden = jnp.einsum('bid,bde->bie', keys, weight, precision=HIGH) + bias[:, None, :]
    center = hidden - lax.optimization_barrier(jnp.mean(hidden, -1, keepdims=True))
    scale = lax.rsqrt(lax.optimization_barrier(jnp.mean(center * center, -1, keepdims=True)) + epsilon)
    normed = center * scale
    misfit = (gamma[:, None, :] * normed + beta[:, None, :] - (values - keys)) * keep[:, :, None]
    scaled = misfit * gamma[:, None, :]
    slope = scale * (scaled - lax.optimization_barrier(jnp.mean(scaled, -1, keepdims=True)) - normed * lax.optimization_barrier(jnp.mean(scaled * normed, -1, keepdims=True)))
    order = jnp.arange(size)
    lower = (order[None, :] <= order[:, None]).astype(jnp.float32)
    coupling = lower[None] * rate[:, None, :] / (order[:, None].astype(jnp.float32) + 1.0)[None]
    intersection = jnp.einsum('bjd,bid->bji', query, keys, precision=HIGH) + 1.0
    answer = jnp.einsum('bjd,bde->bje', query, weight, precision=HIGH) + bias[:, None, :]
    answer = answer - jnp.einsum('bji,bie->bje', coupling * intersection, slope, precision=HIGH)
    last_rate = rate / size
    weight = weight - jnp.einsum('bid,bie->bde', keys * last_rate[:, :, None], slope, precision=HIGH)
    bias = bias - jnp.einsum('bi,bie->be', last_rate, slope, precision=HIGH)
    result = query + gamma[:, None, :] * center_scale(answer) + beta[:, None, :]
    return ((weight, bias), result)

def mixer_core(projected, rate_logits, keep, init_weight, init_bias, gamma, beta):
    groups, length, triple = projected.shape
    heads = rate_logits.shape[-1]
    head_size = init_weight.shape[1]
    width = heads * head_size
    count = groups * heads
    blocks = length // MINI

    def split_heads(matrix):
        return matrix.reshape(groups, length, heads, head_size).transpose(0, 2, 1, 3).reshape(count, length, head_size)

    def tile(vector):
        return jnp.broadcast_to(vector.reshape(heads, head_size)[None], (groups, heads, head_size)).reshape(count, head_size)

    def cut(matrix):
        return matrix.reshape(count, blocks, MINI, head_size).transpose(1, 0, 2, 3)

    def cut_flat(matrix):
        return matrix.reshape(count, blocks, MINI).transpose(1, 0, 2)
    query = split_heads(projected[:, :, :width])
    keys = split_heads(projected[:, :, width:2 * width])
    values = split_heads(projected[:, :, 2 * width:])
    rate = inner_rate / head_size * jax.nn.sigmoid(rate_logits)
    rate = rate.transpose(0, 2, 1).reshape(count, length)
    keep_all = jnp.broadcast_to(keep[:, None, :], (groups, heads, length)).reshape(count, length)
    weight = jnp.broadcast_to(init_weight.reshape(heads, head_size, head_size)[None], (groups, heads, head_size, head_size))
    weight = weight.reshape(count, head_size, head_size)
    gamma_all = tile(gamma)
    beta_all = tile(beta)

    def advance(state, item):
        return inner_step(state, item, gamma_all, beta_all)
    final_state, pieces = lax.scan(jax.checkpoint(advance), (weight, tile(init_bias)), (cut(query), cut(keys), cut(values), cut_flat(rate), cut_flat(keep_all)))
    merged = pieces.transpose(1, 0, 2, 3).reshape(groups, heads, length, head_size).transpose(0, 2, 1, 3)
    return merged.reshape(groups, length, width)

def forward(inputs, lengths, attn_gain, w_qkv, w_lr, init_w, init_b, inner_gain, inner_bias, post_gain, w_out, ffn_gain, w_gate, w_up, w_down):
    groups, length, width = inputs.shape
    rows = inputs.reshape(groups * length, width)
    normed = low(rms_scale(rows) * attn_gain)
    projected = low_back(jnp.dot(normed, w_qkv, precision=HIGH))
    rate_logits = low_back(jnp.dot(normed, w_lr, precision=HIGH))
    keep = (jnp.arange(length)[None, :] < lengths[:, None]).astype(jnp.float32)
    mixed = mixer_core(projected.reshape(groups, length, -1), rate_logits.reshape(groups, length, -1), keep, init_w, init_b, inner_gain, inner_bias).reshape(groups * length, width)
    posted = low(rms_scale(mixed) * post_gain)
    branch = low_back(jnp.dot(posted, w_out, precision=HIGH))
    middle = rows + branch
    ffn_in = low(rms_scale(middle) * ffn_gain)
    gate = low_back(jnp.dot(ffn_in, w_gate, precision=HIGH))
    upper = low_back(jnp.dot(ffn_in, w_up, precision=HIGH))
    hidden = low(jax.nn.silu(gate) * upper)
    result = middle + low_back(jnp.dot(hidden, w_down, precision=HIGH))
    return result.reshape(groups, length, width)

def reference(tokens, lengths, attn_gain, w_qkv, w_lr, init_w, init_b, inner_gain, inner_bias, post_gain, w_out, ffn_gain, w_gate, w_up, w_down, d_out):
    params = tuple((p.astype(jnp.float32) for p in (attn_gain, w_qkv, w_lr, init_w, init_b, inner_gain, inner_bias, post_gain, w_out, ffn_gain, w_gate, w_up, w_down)))
    group = math.gcd(SEQS, max(1, 4096 // TOK_DEV))
    steps_count = SEQS // group
    inputs = tokens.astype(jnp.float32).reshape(steps_count, group, TOK_DEV, D)
    seq_lengths = lengths.reshape(steps_count, group)
    cotangent = d_out.astype(jnp.float32).reshape(steps_count, group, TOK_DEV, D)

    def advance(total, item):
        span_in, span_lengths, span_cot = item

        def apply(values, *weights):
            return forward(values, span_lengths, *weights)
        result, pull = jax.vjp(apply, span_in, *params)
        grads = pull(span_cot)
        total = tuple((t + g for t, g in zip(total, grads[1:])))
        return (total, (result, grads[0]))
    zeros = tuple((jnp.zeros_like(p) for p in params))
    total, (results, input_grads) = lax.scan(advance, zeros, (inputs, seq_lengths, cotangent))
    output = results.reshape(TOKENS, D).astype(jnp.bfloat16)
    return (output, input_grads.reshape(TOKENS, D), total[0], total[1], total[2], total[3], total[4], total[5], total[6], total[7], total[8], total[9], total[10], total[11], total[12])
```

```python
import functools

import jax
import jax.numpy as jnp
from jax import lax
from jax.experimental import pallas as pl
from jax.experimental.pallas import tpu as pltpu
from jax.sharding import PartitionSpec as P

BF, F32 = jnp.bfloat16, jnp.float32
MESH = pl.DeviceIdType.MESH
EPS = 1e-6
D, T, FF, FB = 1024, 128, 2736, 384
NN, NT, TN = ((1,), (0,)), ((1,), (1,)), ((0,), (0,))
VMEM = pl.BlockSpec(memory_space=pltpu.VMEM)
HBM = pl.BlockSpec(memory_space=pl.ANY)
LR, ATTN, INITB, IGAIN, IBIAS, POST, FFN, LEN = 64, 80, 81, 82, 83, 84, 85, 86


def dot(a, b, dims):
    return lax.dot_general(a, b, (dims, ((), ())), preferred_element_type=F32)


class Place:
    def __init__(self):
        dp, fs = lax.axis_index("dp"), lax.axis_index("fsdp")
        self.x = (dp // 2) * 2 + fs % 2
        self.c = dp % 2
        self.y = fs // 8
        self.z = (fs // 2) % 4
        self.p = self.x * 2 + self.c

    def dev(self, x=None, c=None, y=None, z=None):
        x = self.x if x is None else x
        c = self.c if c is None else c
        y = self.y if y is None else y
        z = self.z if z is None else z
        return ((x // 2) * 2 + c, y * 8 + z * 2 + x % 2)

    def group(self, k):
        q = (self.p + k) % 8
        return q, self.dev(x=q // 2, c=q % 2)

    def ring(self, k):
        return self.dev(x=(self.x + k) % 4)

    def sibling(self):
        return self.dev(c=1 - self.c)

    def along_y(self, k):
        return self.dev(y=(self.y + k) % 4)

    def along_z(self, k):
        return self.dev(z=(self.z + k) % 4)


def greet(peers):
    barrier = pltpu.get_barrier_semaphore()
    for peer in peers:
        pl.semaphore_signal(barrier, inc=1, device_id=peer, device_id_type=MESH)
    pl.semaphore_wait(barrier, len(peers))


def group_peers(me):
    return [me.group(k)[1] for k in range(1, 8)]


def plane_peers(me):
    return [me.along_y(k) for k in (1, 2, 3)] + [me.along_z(k) for k in (1, 2, 3)]


def remote(src, dst, send, recv, peer):
    return pltpu.make_async_remote_copy(
        src_ref=src, dst_ref=dst, send_sem=send, recv_sem=recv, device_id=peer, device_id_type=MESH
    )


class GroupGather:
    def __init__(self, me, src, dst, send, recv, local):
        self.me, self.dst, self.send, self.recv = me, dst, send, recv
        self.own = pltpu.make_async_copy(src, dst.at[me.p], local)
        self.out = [
            remote(src, dst.at[me.p], send.at[k], recv.at[k], me.sibling() if k == 0 else me.ring(k))
            for k in (0, 1, 3, 2)
        ]

    def start(self):
        self.own.start()
        for cp in self.out:
            cp.start()

    def forward(self):
        me = self.me
        self.passed = []
        for n, k in enumerate((0, 1, 3, 2)):
            self.out[n].wait_recv()
            if k:
                q = ((me.x + 4 - k) % 4) * 2 + me.c
                cp = remote(
                    self.dst.at[q], self.dst.at[q], self.send.at[3 + k], self.recv.at[3 + k], me.sibling()
                )
                cp.start()
                self.passed.append(cp)

    def finish(self):
        for cp in self.passed:
            cp.wait_recv()
        for cp in self.out + self.passed:
            cp.wait_send()
        self.own.wait()


GATHER_SEMS = [pltpu.SemaphoreType.DMA((7,)), pltpu.SemaphoreType.DMA((7,)), pltpu.SemaphoreType.DMA]


class PlaneGather:
    def __init__(self, me, chunk, whole, y_first, send, recv, local):
        y, z = me.y, me.z
        first, second = (me.along_y, me.along_z) if y_first else (me.along_z, me.along_y)
        self.own = pltpu.make_async_copy(chunk, whole.at[:, y, z], local)
        self.one = [
            remote(chunk, whole.at[:, y, z], send.at[k - 1], recv.at[k - 1], first(k)) for k in (1, 3, 2)
        ]
        line = whole.at[:, :, z] if y_first else whole.at[:, y]
        self.two = [remote(line, line, send.at[k + 2], recv.at[k + 2], second(k)) for k in (1, 3, 2)]

    def start(self):
        self.own.start()
        for cp in self.one:
            cp.start()

    def middle(self):
        self.own.wait()
        for cp in self.one:
            cp.wait_recv()
        for cp in self.two:
            cp.start()

    def finish(self):
        for cp in self.two:
            cp.wait_recv()
        for cp in self.one + self.two:
            cp.wait_send()


PLANE_SEMS = [pltpu.SemaphoreType.DMA((6,)), pltpu.SemaphoreType.DMA((6,)), pltpu.SemaphoreType.DMA]


class GroupReduce:
    def __init__(self, me, parts, sib, acc, blocks, send, recv):
        self.me, self.parts, self.sib, self.acc, self.blocks = me, parts, sib, acc, blocks
        self.over, self.ring = [], []
        for k in (2, 1, 3, 0):
            to = (me.x + k) % 4
            self.over.append(
                remote(parts.at[to * 2 + 1 - me.c], sib.at[k], send.at[k], recv.at[k], me.sibling())
            )
            if k:
                self.ring.append(remote(acc.at[k], blocks.at[k], send.at[3 + k], recv.at[3 + k], me.ring(k)))

    def start(self):
        for cp in self.over:
            cp.start()

    def middle(self):
        me = self.me
        for n, k in enumerate((2, 1, 3, 0)):
            self.over[n].wait_recv()
            mine = self.parts[((me.x + k) % 4) * 2 + me.c].astype(F32)
            total = (mine + self.sib[k].astype(F32)).astype(BF)
            if k:
                self.acc[k] = total
                self.ring[n].start()
            else:
                self.blocks[0] = total

    def finish(self):
        for cp in self.ring:
            cp.wait_recv()
        for cp in self.over + self.ring:
            cp.wait_send()


REDUCE_SEMS = [pltpu.SemaphoreType.DMA((7,)), pltpu.SemaphoreType.DMA((7,))]


class PlaneReduce:
    def __init__(self, me, whole, cols, z_first, got1, part, got2, total, send, recv):
        self.me, self.z_first = me, z_first
        lo, n = cols
        self.view = lambda y, z: whole[:, y, z, :, lo : lo + n]
        self.got1, self.part, self.got2, self.total, self.cols = got1, part, got2, total, cols
        self.one, self.two = [], []
        for k in (1, 3, 2):
            if z_first:
                src, peer = whole.at[:, :, (me.z + k) % 4, :, lo : lo + n], me.along_z(k)
            else:
                src, peer = whole.at[:, (me.y + k) % 4, :, :, lo : lo + n], me.along_y(k)
            self.one.append(remote(src, got1.at[k - 1], send.at[k - 1], recv.at[k - 1], peer))
            to, peer = ((me.y + k) % 4, me.along_y(k)) if z_first else ((me.z + k) % 4, me.along_z(k))
            self.two.append(remote(part.at[to], got2.at[k - 1], send.at[k + 2], recv.at[k + 2], peer))

    def start(self):
        for cp in self.one:
            cp.start()

    def middle(self):
        me = self.me
        for cp in self.one:
            cp.wait_recv()

        def add(i, carry):
            mine = self.view(i, me.z) if self.z_first else self.view(me.y, i)
            s = mine.astype(F32)
            for k in range(3):
                s = s + self.got1[k, :, i].astype(F32)
            self.part[i] = s.astype(BF)
            return carry

        lax.fori_loop(0, 4, add, 0)
        for cp in self.two:
            cp.start()

    def finish(self):
        for cp in self.two:
            cp.wait_recv()
        lo, n = self.cols
        s = self.part[self.me.y if self.z_first else self.me.z].astype(F32)
        for k in range(3):
            s = s + self.got2[k].astype(F32)
        self.total[:, :, lo : lo + n] = s
        for cp in self.one + self.two:
            cp.wait_send()


def plane_reduce_scratch(n):
    return [
        pltpu.VMEM((3, 4, 4, 16, n), BF),
        pltpu.VMEM((4, 4, 16, n), BF),
        pltpu.VMEM((3, 4, 16, n), BF),
        pltpu.SemaphoreType.DMA((6,)),
        pltpu.SemaphoreType.DMA((6,)),
    ]


def row_exchange(me, total, got, send, recv, local):
    def rows(q):
        x, c = q // 2, q % 2
        return total.at[(x // 2) * 2 + c, pl.ds(pl.multiple_of((x % 2) * 8, 8), 8)]

    own = pltpu.make_async_copy(rows(me.p), got.at[me.p], local)
    out = []
    for k in range(1, 8):
        q, peer = me.group(k)
        out.append(remote(rows(q), got.at[me.p], send.at[k - 1], recv.at[k - 1], peer))
    return own, out


EXCHANGE_SEMS = [pltpu.SemaphoreType.DMA((7,)), pltpu.SemaphoreType.DMA((7,)), pltpu.SemaphoreType.DMA]


def start_all(cps):
    for cp in cps:
        cp.start()


def wait_all(cps):
    for cp in cps:
        cp.wait()


def start_kernel(
    wq, small, wo, wg, wu, wd, tok, dout,
    wa_out, wo_out, wf_chunk, tok_all, dout_all,
    pad, sendbuf, recvbuf, chunk_a, chunk_o,
    a_send, a_recv,
    t_send, t_recv, t_loc, d_send, d_recv, d_loc,
    pa_send, pa_recv, pa_loc, po_send, po_recv, po_loc, o_send, o_recv,
):
    me = Place()
    greet(group_peers(me) + plane_peers(me))

    for n, w in enumerate((wg, wu, wd)):
        pad[n, :, FF - FF % 128 :] = jnp.zeros((8, 8 * FB - (FF - FF % 128)), F32)
        pad[n, :, :FF] = w[...].astype(F32)
    low = small[...].astype(F32)
    for q in range(8):
        def cols(ref, at, n):
            return ref[:, at : at + n].astype(F32)

        def put(at, top, bottom):
            sendbuf[q, :, at : at + top.shape[1]] = jnp.concatenate([top, bottom], 0).astype(BF)

        put(0, cols(wq, 128 * q, 128), cols(wq, 2048 + 128 * q, 128))
        put(128, cols(wq, 1024 + 128 * q, 128), low)
        half = 512 * (q % 2)
        put(256, cols(wo, half, 256), cols(wo, half + 256, 256))
        put(512, pad[0, :, FB * q : FB * q + FB], pad[1, :, FB * q : FB * q + FB])
        put(
            896,
            pad[2, :, FB * q : FB * q + 256],
            jnp.concatenate([pad[2, :, FB * q + 256 : FB * q + FB], jnp.zeros((8, 128), F32)], 1),
        )

    sends = []
    for k in range(1, 8):
        q, peer = me.group(k)
        sends.append(remote(sendbuf.at[q], recvbuf.at[me.p], a_send.at[k - 1], a_recv.at[k - 1], peer))
    start_all(sends)
    g_tok = GroupGather(me, tok, tok_all, t_send, t_recv, t_loc)
    g_dout = GroupGather(me, dout, dout_all, d_send, d_recv, d_loc)
    g_tok.start()
    recvbuf[me.p] = sendbuf[me.p]
    for cp in sends:
        cp.wait_recv()
    for dp in range(4):
        p0 = (dp // 2) * 4 + dp % 2
        r0, r1 = recvbuf[p0].astype(F32), recvbuf[p0 + 2].astype(F32)

        def top(lo, n):
            return jnp.concatenate([r0[:8, lo : lo + n], r1[:8, lo : lo + n]], 0).astype(BF)

        def bottom(lo, n):
            return jnp.concatenate([r0[8:, lo : lo + n], r1[8:, lo : lo + n]], 0).astype(BF)

        chunk_a[dp, :, :128] = top(0, 128)
        chunk_a[dp, :, 128:256] = top(128, 128)
        chunk_a[dp, :, 256:384] = bottom(0, 128)
        chunk_a[dp, :, 384:512] = bottom(128, 128)
        chunk_o[dp, :, :256] = top(256, 256)
        chunk_o[dp, :, 256:512] = bottom(256, 256)
        wf_chunk[dp, :, :FB] = top(512, FB)
        wf_chunk[dp, :, FB : 2 * FB] = bottom(512, FB)
        wf_chunk[dp, :, 2 * FB : 2 * FB + 256] = top(896, 256)
        wf_chunk[dp, :, 2 * FB + 256 :] = bottom(896, 128)
    pa = PlaneGather(me, chunk_a, wa_out, True, pa_send, pa_recv, pa_loc)
    po = PlaneGather(me, chunk_o, wo_out.at[me.c], False, po_send, po_recv, po_loc)
    pa.start()
    po.start()
    g_dout.start()
    pa.middle()
    po.middle()
    g_tok.forward()
    po.finish()
    over = remote(wo_out.at[me.c], wo_out.at[me.c], o_send, o_recv, me.sibling())
    over.start()
    pa.finish()
    g_dout.forward()
    g_tok.finish()
    g_dout.finish()
    over.wait()
    for cp in sends:
        cp.wait_send()


def turn_kernel(mixed, full, send, recv, local):
    me = Place()
    greet(group_peers(me))
    here = full.at[:, pl.ds(pl.multiple_of(me.p * 128, 128), 128)]
    own = pltpu.make_async_copy(mixed.at[me.p], here, local)
    own.start()
    out = []
    for k in range(1, 8):
        q, peer = me.group(k)
        out.append(remote(mixed.at[q], here, send.at[k - 1], recv.at[k - 1], peer))
    start_all(out)
    wait_all(out)
    own.wait()


def feed_kernel(x, chunk, x_all, whole, gs, gr, gl, as_, ar, al, bs, br, bl):
    me = Place()
    greet(group_peers(me) + plane_peers(me))
    g = GroupGather(me, x, x_all, gs, gr, gl)
    a = PlaneGather(me, chunk.at[:, :, :640], whole.at[:, :, :, :, :640], True, as_, ar, al)
    b = PlaneGather(me, chunk.at[:, :, 640:], whole.at[:, :, :, :, 640:], False, bs, br, bl)
    a.start()
    b.start()
    g.start()
    a.middle()
    b.middle()
    g.forward()
    g.finish()
    a.finish()
    b.finish()


def reduce_kernel(
    dx, out, grads, dx_blocks, out_blocks, total,
    dx_sib, dx_acc, out_sib, out_acc, ds, dr, os_, or_,
    a1, ap, a2, as_, ar, b1, bp, b2, bs, br,
):
    me = Place()
    greet(group_peers(me) + plane_peers(me))
    one = GroupReduce(me, dx, dx_sib, dx_acc, dx_blocks, ds, dr)
    two = GroupReduce(me, out, out_sib, out_acc, out_blocks, os_, or_)
    a = PlaneReduce(me, grads, (0, 640), True, a1, ap, a2, total, as_, ar)
    b = PlaneReduce(me, grads, (640, 512), False, b1, bp, b2, total, bs, br)
    one.start()
    a.start()
    b.start()
    two.start()
    one.middle()
    two.middle()
    a.middle()
    b.middle()
    one.finish()
    a.finish()
    b.finish()
    two.finish()


def spread_kernel(d_mixed, total, parts, got, send, recv, local, es, er, el):
    me = Place()
    greet(group_peers(me))
    own = pltpu.make_async_copy(
        d_mixed.at[:, pl.ds(pl.multiple_of(me.p * 128, 128), 128)], parts.at[me.p], local
    )
    own.start()
    out = []
    for k in range(1, 8):
        q, peer = me.group(k)
        cols = d_mixed.at[:, pl.ds(pl.multiple_of(q * 128, 128), 128)]
        out.append(remote(cols, parts.at[me.p], send.at[k - 1], recv.at[k - 1], peer))
    start_all(out)
    mine, rows = row_exchange(me, total, got, es, er, el)
    mine.start()
    start_all(rows)
    wait_all(out)
    own.wait()
    wait_all(rows)
    mine.wait()


def last_kernel(
    dn, ga, go, blocks, got_a, got_o,
    sib, acc, ns, nr, o_sib, o_sum, xs, xr, tot_a, tot_o,
    a1, ap, a2, as_, ar, b1, bp, b2, bs, br, eas, ear, eal, eos, eor, eol,
):
    me = Place()
    greet(group_peers(me) + plane_peers(me))
    over = remote(go.at[1 - me.c], o_sib, xs, xr, me.sibling())
    over.start()
    g = GroupReduce(me, dn, sib, acc, blocks, ns, nr)
    a = PlaneReduce(me, ga, (0, 512), True, a1, ap, a2, tot_a, as_, ar)
    b = PlaneReduce(me, o_sum, (0, 512), False, b1, bp, b2, tot_o, bs, br)
    a.start()
    g.start()
    over.wait_recv()

    def add(i, carry):
        for j in range(4):
            o_sum[i, j] = (go[me.c, i, j].astype(F32) + o_sib[i, j].astype(F32)).astype(BF)
        return carry

    lax.fori_loop(0, 4, add, 0)
    b.start()
    g.middle()
    a.middle()
    b.middle()
    a.finish()
    mine_a, rows_a = row_exchange(me, tot_a, got_a, eas, ear, eal)
    mine_a.start()
    start_all(rows_a)
    b.finish()
    mine_o, rows_o = row_exchange(me, tot_o, got_o, eos, eor, eol)
    mine_o.start()
    start_all(rows_o)
    g.finish()
    over.wait_send()
    wait_all(rows_a)
    wait_all(rows_o)
    mine_a.wait()
    mine_o.wait()


def iota(shape, dim):
    return lax.broadcasted_iota(jnp.int32, shape, dim)


def same_head():
    return (iota((128, 128), 0) < 64) == (iota((128, 128), 1) < 64)


def split(v):
    hi = v.astype(BF)
    return hi, (v - hi.astype(F32)).astype(BF)


def averager():
    j = jnp.where(same_head(), 1.0 / 64, 0.0).astype(BF)
    return jnp.concatenate([j, j], 0)


def means(v, avg):
    return dot(jnp.concatenate(split(v), 1), avg, NN)


def stack(v):
    v = v.astype(F32)
    first = iota(v.shape, 1) < 64
    return jnp.concatenate([jnp.where(first, v, 0.0), jnp.where(first, 0.0, v)], 0).astype(BF)


def fine(a, b, dims=NN):
    ah, al = split(a)
    bh, bl = split(b)
    return dot(ah, bh, dims) + dot(al, bh, dims) + dot(ah, bl, dims)


def masks():
    row, col = iota((128, 256), 0), iota((128, 256), 1) % 128
    br, bc = row // 16, col // 16
    earlier = jnp.where(bc < br, 1.0 / 16, 0.0)
    later = jnp.where(bc > br, 1.0 / 16, 0.0)
    low = earlier + jnp.where((bc == br) & (col <= row), 1.0 / (row % 16 + 1).astype(F32), 0.0)
    up = later + jnp.where((bc == br) & (row <= col), 1.0 / (col % 16 + 1).astype(F32), 0.0)
    return earlier, later, low, up


def head_params(wa_ref, p):
    mine = wa_ref[pl.ds(pl.multiple_of(p * 128, 128), 128), FB:].astype(F32)
    rows = mine.T
    both = jnp.where(iota((128, 128), 1) < 64, mine, pltpu.roll(mine, 64, 1))
    w0 = jnp.where(same_head(), both, 0.0)
    return w0, rows[INITB : INITB + 1], rows[IGAIN : IGAIN + 1], rows[IBIAS : IBIAS + 1]


def group_place():
    dp, fs = lax.axis_index("dp"), lax.axis_index("fsdp")
    return ((dp // 2) * 2 + fs % 2) * 2 + dp % 2, fs // 2


def keep_rows(wa_ref, f, b):
    x, c = b // 2, b % 2
    rows = wa_ref[pl.ds(pl.multiple_of(((x // 2) * 2 + c) * 256 + f * 16, 16), 16), FB:].astype(F32)
    row = rows[(x % 2) * 8 : (x % 2) * 8 + 1]
    length = jnp.sum(jnp.where(iota((1, 128), 1) == LEN, row, 0.0), 1, keepdims=True)
    return jnp.where(iota((128, 128), 0).astype(F32) < length, 1.0, 0.0)


def rate_of(proj_ref, p):
    col = iota((128, 128), 1)
    pick = jnp.where(iota((128, 128), 0) == LR + 2 * p + jnp.where(col < 64, 0, 1), 1.0, 0.0).astype(BF)
    logits = dot(jnp.concatenate(split(proj_ref[:, FB:]), 1), jnp.concatenate([pick, pick], 0), NN)
    return (1.0 / 64) * jax.nn.sigmoid(logits)


def mix_kernel(tok, wa, normed, proj, mixed, z_out, a_out, ma, mb, zb, gt, mgt, kp, rt, g2):
    p, f = group_place()
    gain = wa[:, FB:].astype(F32).T[ATTN : ATTN + 1]
    avg = averager()

    def project(i, carry):
        rows = tok[pl.ds(i * 2, 2)].reshape(256, D).astype(F32)
        scale = lax.rsqrt(jnp.mean(rows * rows, -1, keepdims=True) + EPS)
        at = pl.ds(pl.multiple_of(i * 256, 256), 256)
        normed[at] = (rows * scale * gain).astype(BF)
        proj[at] = dot(normed[at], wa[...], NN)
        return carry

    lax.fori_loop(0, 4, project, 0)
    w0, b0, gamma, beta = head_params(wa, p)
    w0 = w0 - jnp.where(same_head(), means(w0, avg), 0.0)
    b0 = b0 - means(jnp.broadcast_to(b0, (8, 128)), avg)[:1]
    gamma2 = gamma * gamma
    earlier, _, low, _ = masks()
    rt[...] = rate_of(proj, p)
    for b in range(8):
        kp[b * 128 : b * 128 + 128] = keep_rows(wa, f, b)

    def prepare(b, carry):
        at = pl.ds(pl.multiple_of(b * 128, 128), 128)
        q, k, v = proj[at, :128], proj[at, 128:256], proj[at, 256:384]
        k2 = stack(k)
        ma[b] = ((dot(k.astype(BF), k2, NT) + 1.0) * earlier).astype(BF)
        mb[b] = ((dot(q.astype(BF), k2, NT) + 1.0) * low).astype(BF)
        zb[at] = fine(k, w0) + b0
        a_out[at] = fine(q, w0) + b0
        gt[at] = gamma * (beta - v + k)
        g2[b] = jnp.zeros((256, 128), BF)
        return carry

    lax.fori_loop(0, 8, prepare, 0)
    mgt[...] = means(gt[...], avg)

    def step_rows(ref, t):
        return jnp.concatenate([ref[b * 128 + t * 16 : b * 128 + t * 16 + 16] for b in range(8)], 0)

    for t in range(8):
        z = step_rows(zb, t)
        if t:
            z = z - jnp.concatenate([dot(ma[b, t * 16 : t * 16 + 16], g2[b], NN) for b in range(8)], 0)
        gtt, keep, rate = step_rows(gt, t), step_rows(kp, t), step_rows(rt, t)
        gz = gamma2 * z
        m = means(jnp.concatenate([z * z, gz, gz * z, gtt * z], 0), avg)
        s = lax.rsqrt(m[:128] + EPS)
        n = z * s
        mu = keep * (s * m[128:256] + step_rows(mgt, t))
        mun = keep * s * (s * m[256:384] + m[384:])
        h = keep * (gamma2 * n + gtt) - mu - n * mun
        g = stack(rate * s * h)
        for b in range(8):
            z_out[b * 128 + t * 16 : b * 128 + t * 16 + 16] = z[b * 16 : b * 16 + 16]
            g2[b, t * 16 : t * 16 + 16] = g[b * 16 : b * 16 + 16]
            g2[b, 128 + t * 16 : 144 + t * 16] = g[128 + b * 16 : 144 + b * 16]

    def answer(b, carry):
        at = pl.ds(pl.multiple_of(b * 128, 128), 128)
        a = a_out[at] - dot(mb[b], g2[b], NN)
        a_out[at] = a
        na = a * lax.rsqrt(means(a * a, avg) + EPS)
        mixed[b] = (proj[at, :128] + gamma * na + beta).astype(BF)
        return carry

    lax.fori_loop(0, 8, answer, 0)


def rms(v):
    return lax.rsqrt(jnp.mean(v * v, -1, keepdims=True) + EPS)


def rms_back(v, gain, dy):
    r = rms(v)
    n = v * r
    inner = dy * gain
    return r * (inner - n * jnp.mean(inner * n, -1, keepdims=True)), jnp.sum(dy * n, 0, keepdims=True)


def join_kernel(mixed, tok, wo, wa, posted, middle, ffn_in):
    vecs = wa[:, FB:].astype(F32).T
    m = mixed[...].astype(F32)
    posted[...] = (m * rms(m) * vecs[POST : POST + 1]).astype(BF)
    for h in range(2):
        at = slice(512 * h, 512 * h + 512)
        middle[:, at] = tok[:, at].astype(F32) + dot(posted[...], wo[h], NN)
    mid = middle[...]
    ffn_in[...] = (mid * rms(mid) * vecs[FFN : FFN + 1]).astype(BF)


def ffn_kernel(x, dout, wf, out, dx, grads, hidden, dgu):
    wg, wu, wd = (slice(FB * n, FB * n + FB) for n in range(3))

    def rows(i, carry):
        two = pl.ds(i * 2, 2)
        at = pl.ds(pl.multiple_of(i * 256, 256), 256)
        xi = x[two].reshape(256, D)
        gate = dot(xi, wf[:, wg], NN)
        upper = dot(xi, wf[:, wu], NN)
        sigma = jax.nn.sigmoid(gate)
        active = gate * sigma
        hid = (active * upper).astype(BF)
        hidden[at] = hid
        out[two] = dot(hid, wf[:, wd], NT).astype(BF).reshape(2, T, D)
        dh = dot(dout[two].reshape(256, D), wf[:, wd], NN)
        dg = (dh * upper * (sigma + active * (1.0 - sigma))).astype(BF)
        du = (dh * active).astype(BF)
        dgu[at, :FB] = dg
        dgu[at, FB:] = du
        dx[two] = (dot(dg, wf[:, wg], NT) + dot(du, wf[:, wu], NT)).astype(BF).reshape(2, T, D)
        return carry

    lax.fori_loop(0, 4, rows, 0)
    for i in range(4):
        at = slice(256 * i, 256 * i + 256)
        grads[at, : 2 * FB] = dot(x[:, :, at].reshape(8 * T, 256), dgu[...], TN).astype(BF)
        grads[at, 2 * FB :] = dot(dout[:, :, at].reshape(8 * T, 256), hidden[...], TN).astype(BF)


def part_kernel(dx_blocks, out_blocks, middle, posted, mixed, dout, wo, wa, output, d_middle, d_mixed, g_out, vec, dbr):
    vecs = wa[:, FB:].astype(F32).T

    def total(ref):
        return ((ref[0].astype(F32) + ref[1].astype(F32)) + (ref[2].astype(F32) + ref[3].astype(F32)))

    mid = middle[...]
    output[...] = (mid + total(out_blocks)).astype(BF)
    dn, g_ffn = rms_back(mid, vecs[FFN : FFN + 1], total(dx_blocks))
    dm = dout[...].astype(F32) + dn
    d_middle[...] = dm
    dbr[...] = dm.astype(BF)
    for h in range(2):
        g_out[h] = dot(posted[...], dbr[:, 512 * h : 512 * h + 512], TN).astype(BF)
    d_posted = dot(dbr[:, :512], wo[0], NT) + dot(dbr[:, 512:], wo[1], NT)
    dmix, g_post = rms_back(mixed[...].astype(F32), vecs[POST : POST + 1], d_posted)
    d_mixed[...] = dmix.astype(BF)
    vec[...] = jnp.concatenate([g_ffn, g_post, jnp.zeros((6, D), F32)], 0)


def back_kernel(
    dmix, tok, wa, normed, proj, z_in, a_in, vec,
    dn, grads,
    rt, kp, s_, n_, u_, h_, mun_, mg1, mg2, da_, dgb, dz_, du_, dgp, mat, dz2, dp, sums,
):
    p, f = group_place()
    avg = averager()
    w0, _, gamma, beta = head_params(wa, p)
    w0 = w0 - jnp.where(same_head(), means(w0, avg), 0.0)
    gamma2 = gamma * gamma
    earlier, later, low, up = masks()
    rt[...] = rate_of(proj, p)
    for b in range(8):
        kp[b * 128 : b * 128 + 128] = keep_rows(wa, f, b)
    sums[...] = jnp.zeros((8, 128), F32)

    def prepare(b, carry):
        at = pl.ds(pl.multiple_of(b * 128, 128), 128)
        q, k, v = proj[at, :128], proj[at, 128:256], proj[at, 256:384]
        z, keep = z_in[at], kp[at]
        s = lax.rsqrt(means(z * z, avg) + EPS)
        n = z * s
        gn = gamma2 * n
        u = keep * (gn + gamma * (beta - v + k))
        m = means(jnp.concatenate([u, u * n, gn, gn * n], 0), avg)
        s_[at], n_[at], u_[at] = s, n, u
        h_[at] = u - m[:128] - n * m[128:256]
        mun_[at], mg1[at], mg2[at] = m[128:256], m[256:384], m[384:]
        a = a_in[at]
        sa = lax.rsqrt(means(a * a, avg) + EPS)
        na = a * sa
        d = dmix[b].astype(F32)
        dna = d * gamma
        da = sa * (dna - na * means(dna * na, avg))
        da_[at] = da
        sums[0:1] += jnp.sum(d * na, 0, keepdims=True)
        sums[1:2] += jnp.sum(d, 0, keepdims=True)
        kb = k.astype(BF)
        mbt = ((dot(kb, stack(q), NT) + 1.0) * up).astype(BF)
        dgb[at] = -dot(mbt, stack(da), NN)
        mat[b] = ((dot(kb, stack(k), NT) + 1.0) * later).astype(BF)
        dz2[b] = jnp.zeros((256, 128), BF)
        return carry

    lax.fori_loop(0, 8, prepare, 0)

    def step_rows(ref, t):
        return jnp.concatenate([ref[b * 128 + t * 16 : b * 128 + t * 16 + 16] for b in range(8)], 0)

    for t in range(7, -1, -1):
        g = step_rows(dgb, t)
        if t < 7:
            g = g - jnp.concatenate([dot(mat[b, t * 16 : t * 16 + 16], dz2[b], NN) for b in range(8)], 0)
        s, n, u, h = step_rows(s_, t), step_rows(n_, t), step_rows(u_, t), step_rows(h_, t)
        mun, keep = step_rows(mun_, t), step_rows(kp, t)
        dh = s * step_rows(rt, t) * g
        dhn = dh * n
        m = means(jnp.concatenate([dh, dhn, dh * h, gamma2 * dhn], 0), avg)
        md, cc = m[:128], m[128:256]
        du = dh - md - cc * n
        mdn = keep * (m[384:] - md * step_rows(mg1, t) - cc * step_rows(mg2, t)) - 2.0 * mun * cc
        dn_ = keep * gamma2 * du - mun * dh - cc * u
        dz = s * (dn_ - n * (m[256:384] + mdn))
        dzs = stack(dz)
        for b in range(8):
            at, here = slice(b * 128 + t * 16, b * 128 + t * 16 + 16), slice(b * 16, b * 16 + 16)
            dz_[at], du_[at], dgp[at] = dz[here], du[here], g[here]
            dz2[b, t * 16 : t * 16 + 16] = dzs[here]
            dz2[b, 128 + t * 16 : 144 + t * 16] = dzs[128 + b * 16 : 144 + b * 16]

    col, row = iota((128, 128), 1), iota((128, 128), 0)
    place = jnp.where(
        ((row == 0) & (col == LR + 2 * p)) | ((row == 64) & (col == LR + 2 * p + 1)), 1.0, 0.0
    ).astype(BF)

    def finish(b, carry):
        at = pl.ds(pl.multiple_of(b * 128, 128), 128)
        q, k, v = proj[at, :128], proj[at, 128:256], proj[at, 256:384]
        s, n, du, keep, rate = s_[at], n_[at], du_[at], kp[at], rt[at]
        da, dz, g = da_[at], dz_[at], s * h_[at]
        dt = keep * gamma * du
        sums[0:1] += jnp.sum(keep * (2.0 * gamma * n + (beta - v + k)) * du, 0, keepdims=True)
        sums[1:2] += jnp.sum(dt, 0, keepdims=True)
        sums[2:3] += jnp.sum(da + dz, 0, keepdims=True)
        drate = 64.0 * means(dgp[at] * g, avg)
        dl = drate * rate * (1.0 - 64.0 * rate)
        gr = rate * g
        gb, dab, dzb = gr.astype(BF), da.astype(BF), dz.astype(BF)
        g2, k2, da2 = stack(gr), stack(k), stack(da)
        sb = (dot(dab, g2, NT) * low).astype(BF)
        sbt = (dot(gb, da2, NT) * up).astype(BF)
        sa = (dot(dzb, g2, NT) * earlier + dot(gb, dz2[b], NT) * later).astype(BF)
        dq = dmix[b].astype(F32) + fine(da, w0, NT) - dot(sb, k2, NN)
        dk = dt + fine(dz, w0, NT) - dot(sbt, stack(q), NN) - dot(sa, k2, NN)
        dp[at, :128] = dq.astype(BF)
        dp[at, 128:256] = dk.astype(BF)
        dp[at, 256:384] = (-dt).astype(BF)
        dp[at, 384:] = dot(dl.astype(BF), place, NN).astype(BF)
        return carry

    lax.fori_loop(0, 8, finish, 0)
    dw = dot(proj[:, 128:256].astype(BF), dz_[...].astype(BF), TN)
    dw = dw + dot(proj[:, :128].astype(BF), da_[...].astype(BF), TN)
    dw = dw - means(dw, avg)
    dw = jnp.where(row < 64, dw, pltpu.roll(dw, 64, 1))
    dw = jnp.where(col < 64, dw, 0.0)
    sm = sums[...]
    db = sm[2:3] - means(jnp.broadcast_to(sm[2:3], (8, 128)), avg)[:1]
    mine = jnp.where(row == INITB, db, 0.0) + jnp.where(row == IGAIN, sm[0:1], 0.0)
    mine = mine + jnp.where(row == IBIAS, sm[1:2], 0.0)
    mine = dw + mine.T

    attn = jnp.zeros((1, D), F32)
    for i in range(4):
        two = slice(2 * i, 2 * i + 2)
        at = slice(256 * i, 256 * i + 256)
        d = dot(dp[at], wa[...], NT)
        dn[two] = d.astype(BF).reshape(2, T, D)
        v = tok[two].reshape(256, D).astype(F32)
        attn = attn + jnp.sum(d * (v * rms(v)), 0, keepdims=True)
    big = iota((128, D), 0)
    vrows = jnp.where(big == ATTN, attn, 0.0) + jnp.where(big == FFN, vec[0:1], 0.0)
    vrows = vrows + jnp.where(big == POST, vec[1:2], 0.0)
    for i in range(4):
        at = slice(256 * i, 256 * i + 256)
        gr = dot(normed[:, at], dp[...], TN)
        grads[at, :FB] = gr[:, :FB].astype(BF)
        grads[at, FB:] = (gr[:, FB:] + vrows[:, at].T).astype(BF)
    at = pl.ds(pl.multiple_of(p * 128, 128), 128)
    grads[at, FB:] = (grads[at, FB:].astype(F32) + mine).astype(BF)


def end_kernel(blocks, tok, d_middle, wa, got_a, got_o, got_f, d_tok, g_qkv, g_small, g_out, g_gate, g_up, g_down):
    gain = wa[:, FB:].astype(F32).T[ATTN : ATTN + 1]
    dn = (blocks[0].astype(F32) + blocks[1].astype(F32)) + (blocks[2].astype(F32) + blocks[3].astype(F32))
    d, _ = rms_back(tok[...].astype(F32), gain, dn)
    d_tok[...] = d_middle[...] + d
    small = jnp.zeros((8, 128), F32)
    for q in range(8):
        for n in range(3):
            g_qkv[:, 1024 * n + 128 * q : 1024 * n + 128 * q + 128] = got_a[q, :, 128 * n : 128 * n + 128]
        small = small + got_a[q, :, FB:]
        w = min(FB, FF - FB * q)
        for n, ref in enumerate((g_gate, g_up, g_down)):
            ref[:, FB * q : FB * q + w] = got_f[q, :, FB * n : FB * n + w]
    g_small[...] = small
    for h in range(2):
        g_out[:, 512 * h : 512 * h + 512] = (got_o[h] + got_o[2 + h]) + (got_o[4 + h] + got_o[6 + h])


def call(kernel, name, outs, out_specs, scratch, args, in_specs, collective=None, cost=None):
    params = dict(vmem_limit_bytes=60 * 1024 * 1024)
    if collective is not None:
        params.update(collective_id=collective, has_side_effects=True)
    return pl.pallas_call(
        kernel,
        name=name,
        out_shape=[jax.ShapeDtypeStruct(s, d) for s, d in outs],
        in_specs=in_specs,
        out_specs=out_specs,
        scratch_shapes=scratch,
        compiler_params=pltpu.CompilerParams(**params),
    )(*args)


DMA = pltpu.SemaphoreType.DMA


def local(
    tokens, lengths, attn_gain, w_qkv, w_lr, init_w, init_b, inner_gain, inner_bias,
    post_gain, w_out, ffn_gain, w_gate, w_up, w_down, d_out,
):
    vectors = (attn_gain, init_b, inner_gain, inner_bias, post_gain, ffn_gain)
    length = jnp.broadcast_to(lengths.astype(BF).reshape(1, 1), (8, 1))
    small = jnp.concatenate(
        [init_w, w_lr] + [v.reshape(8, 1) for v in vectors] + [length, jnp.zeros((8, 41), BF)], 1
    )
    wa, wo, wf_chunk, tok_all, dout_all = call(
        start_kernel,
        "start",
        [
            ((4, 4, 4, 16, 512), BF), ((2, 4, 4, 4, 16, 512), BF), ((4, 16, 3 * FB), BF),
            ((8, T, D), BF), ((8, T, D), BF),
        ],
        [HBM, HBM, VMEM, HBM, HBM],
        [
            pltpu.VMEM((3, 8, 8 * FB), F32), pltpu.VMEM((8, 16, 1152), BF), pltpu.VMEM((8, 16, 1152), BF),
            pltpu.VMEM((4, 16, 512), BF), pltpu.VMEM((4, 16, 512), BF), DMA((7,)), DMA((7,)),
        ]
        + GATHER_SEMS * 2 + PLANE_SEMS * 2 + [DMA, DMA],
        (w_qkv, small, w_out, w_gate, w_up, w_down.T, tokens, d_out),
        [VMEM] * 6 + [HBM] * 2,
        collective=1,
    )
    wa = wa.reshape(D, 512)
    wo = wo.reshape(2, D, 512)
    big = lambda n, t: pltpu.VMEM((8 * T, n), t)
    normed, proj, mixed, z, a = call(
        mix_kernel,
        "mix",
        [((8 * T, D), BF), ((8 * T, 512), F32), ((8, T, 128), BF), ((8 * T, 128), F32), ((8 * T, 128), F32)],
        [VMEM] * 5,
        [pltpu.VMEM((8, 128, 256), BF)] * 2 + [big(128, F32)] * 5 + [pltpu.VMEM((8, 256, 128), BF)],
        (tok_all, wa),
        [VMEM] * 2,
    )
    (full,) = call(
        turn_kernel, "turn", [((T, D), BF)], [VMEM], EXCHANGE_SEMS, (mixed,), [VMEM], collective=2
    )
    posted, middle, ffn_in = call(
        join_kernel,
        "join",
        [((T, D), BF), ((T, D), F32), ((T, D), BF)],
        [VMEM] * 3,
        [],
        (full, tokens, wo, wa),
        [VMEM] * 4,
    )
    x_all, wf = call(
        feed_kernel,
        "feed",
        [((8, T, D), BF), ((4, 4, 4, 16, 3 * FB), BF)],
        [HBM, HBM],
        GATHER_SEMS + PLANE_SEMS * 2,
        (ffn_in, wf_chunk),
        [HBM, HBM],
        collective=3,
    )
    out, dx, g_ff = call(
        ffn_kernel,
        "ffn",
        [((8, T, D), BF), ((8, T, D), BF), ((D, 3 * FB), BF)],
        [VMEM] * 3,
        [big(FB, BF), big(2 * FB, BF)],
        (x_all, dout_all, wf.reshape(D, 3 * FB)),
        [VMEM] * 3,
    )
    four = pltpu.VMEM((4, T, D), BF)
    dx_blocks, out_blocks, tot_f = call(
        reduce_kernel,
        "reduce",
        [((4, T, D), BF), ((4, T, D), BF), ((4, 16, 3 * FB), F32)],
        [VMEM] * 3,
        [four] * 4 + REDUCE_SEMS * 2 + plane_reduce_scratch(640) + plane_reduce_scratch(512),
        (dx, out, g_ff.reshape(4, 4, 4, 16, 3 * FB)),
        [VMEM] * 3,
        collective=4,
    )
    output, d_middle, d_mixed, g_o, vec = call(
        part_kernel,
        "part",
        [((T, D), BF), ((T, D), F32), ((T, D), BF), ((2, D, 512), BF), ((8, D), F32)],
        [VMEM] * 5,
        [pltpu.VMEM((T, D), BF)],
        (dx_blocks, out_blocks, middle, posted, full, d_out, wo, wa),
        [VMEM] * 8,
    )
    dmix, got_f = call(
        spread_kernel,
        "spread",
        [((8, T, 128), BF), ((8, 8, 3 * FB), F32)],
        [VMEM] * 2,
        EXCHANGE_SEMS * 2,
        (d_mixed, tot_f),
        [VMEM] * 2,
        collective=5,
    )
    dn, g_a = call(
        back_kernel,
        "back",
        [((8, T, D), BF), ((D, 512), BF)],
        [VMEM] * 2,
        [big(128, F32)] * 14
        + [pltpu.VMEM((8, 128, 256), BF), pltpu.VMEM((8, 256, 128), BF), big(512, BF), pltpu.VMEM((8, 128), F32)],
        (dmix, tok_all, wa, normed, proj, z, a, vec),
        [VMEM] * 8,
    )
    blocks, got_a, got_o = call(
        last_kernel,
        "last",
        [((4, T, D), BF), ((8, 8, 512), F32), ((8, 8, 512), F32)],
        [VMEM] * 3,
        [four, four] + REDUCE_SEMS
        + [pltpu.VMEM((4, 4, 4, 16, 512), BF)] * 2 + [DMA, DMA] + [pltpu.VMEM((4, 16, 512), F32)] * 2
        + plane_reduce_scratch(512) * 2 + EXCHANGE_SEMS * 2,
        (dn, g_a.reshape(4, 4, 4, 16, 512), g_o.reshape(2, 4, 4, 4, 16, 512)),
        [VMEM] * 3,
        collective=6,
    )
    d_tok, g_qkv, g_small, g_out, g_gate, g_up, g_down = call(
        end_kernel,
        "end",
        [
            ((T, D), F32), ((8, 3 * D), F32), ((8, 128), F32), ((8, D), F32),
            ((8, FF), F32), ((8, FF), F32), ((8, FF), F32),
        ],
        [VMEM] * 7,
        [],
        (blocks, tokens, d_middle, wa, got_a, got_o, got_f),
        [VMEM] * 7,
    )
    col = lambda n: g_small[:, n]
    return (
        output, d_tok, col(ATTN), g_qkv, g_small[:, LR:ATTN], g_small[:, :LR], col(INITB), col(IGAIN),
        col(IBIAS), col(POST), g_out, col(FFN), g_gate, g_up, g_down.T,
    )


def solution(mesh):
    both = ("dp", "fsdp")
    row, vec, down = P(both, None), P(both), P(None, both)
    return jax.shard_map(
        local,
        mesh=mesh,
        in_specs=(row, vec, vec, row, row, row, vec, vec, vec, vec, row, vec, row, row, down, row),
        out_specs=(row, row, vec, row, row, row, vec, vec, vec, vec, row, vec, row, row, down),
        check_vma=False,
    )
```

```python
import jax
import jax.numpy as jnp
from jax import lax
from jax.experimental import pallas as pl
from jax.experimental.pallas import tpu as pltpu
from jax.sharding import PartitionSpec as P
from types import SimpleNamespace

BF, F32 = jnp.bfloat16, jnp.float32
MESH = pl.DeviceIdType.MESH
EPS = 1e-6
D, T, FF, FB = 1024, 128, 2736, 384
NN, NT, TN = ((1,), (0,)), ((1,), (1,)), ((0,), (0,))
VMEM = pl.BlockSpec(memory_space=pltpu.VMEM)
HBM = pl.BlockSpec(memory_space=pl.ANY)
LR, ATTN, INITB, IGAIN, IBIAS, POST, FFN, LEN = 64, 80, 81, 82, 83, 84, 85, 86


def dot(a, b, dims):
    return lax.dot_general(a, b, (dims, ((), ())), preferred_element_type=F32)


class Place:
    def __init__(self):
        dp, fs = lax.axis_index("dp"), lax.axis_index("fsdp")
        self.x = (dp // 2) * 2 + fs % 2
        self.c = dp % 2
        self.y = fs // 8
        self.z = (fs // 2) % 4
        self.p = self.x * 2 + self.c

    def dev(self, x=None, c=None, y=None, z=None):
        x = self.x if x is None else x
        c = self.c if c is None else c
        y = self.y if y is None else y
        z = self.z if z is None else z
        return ((x // 2) * 2 + c, y * 8 + z * 2 + x % 2)

    def group(self, k):
        q = (self.p + k) % 8
        return q, self.dev(x=q // 2, c=q % 2)

    def ring(self, k):
        return self.dev(x=self.on(k))

    def on(self, k):
        return (self.x + k) % 4

    def back(self, k):
        return (self.x + 4 - k) % 4

    def sibling(self):
        return self.dev(c=1 - self.c)

    def along_y(self, k):
        return self.dev(y=(self.y + k) % 4)

    def along_z(self, k):
        return self.dev(z=(self.z + k) % 4)


def greet(peers):
    barrier = pltpu.get_barrier_semaphore()
    for peer in peers:
        pl.semaphore_signal(barrier, inc=1, device_id=peer, device_id_type=MESH)
    pl.semaphore_wait(barrier, len(peers))


def group_peers(me):
    return [me.group(k)[1] for k in range(1, 8)]


def plane_peers(me):
    return [me.along_y(k) for k in (1, 2, 3)] + [me.along_z(k) for k in (1, 2, 3)]


def remote(src, dst, send, recv, peer):
    return pltpu.make_async_remote_copy(
        src_ref=src, dst_ref=dst, send_sem=send, recv_sem=recv, device_id=peer, device_id_type=MESH
    )


class GroupGather:
    def __init__(self, me, src, dst, send, recv, local):
        self.me, self.dst, self.send, self.recv = me, dst, send, recv
        self.own = pltpu.make_async_copy(src, dst.at[me.p], local)
        self.out = {
            k: remote(src, dst.at[me.p], send.at[k], recv.at[k], me.ring(k) if k else me.sibling())
            for k in (0, 1, 3, 2)
        }
        self.passed = {}

    def start(self):
        self.own.start()
        for cp in self.out.values():
            cp.start()

    def take(self, k):
        self.out[k].wait_recv()
        q = self.me.back(k) * 2 + self.me.c
        at = self.dst.at[q]
        self.passed[k] = remote(at, at, self.send.at[3 + k], self.recv.at[3 + k], self.me.sibling())
        self.passed[k].start()

    def got(self, k):
        if k:
            self.passed[k].wait_recv()
        else:
            self.own.wait()
            self.out[0].wait_recv()

    def done(self):
        for cp in list(self.out.values()) + list(self.passed.values()):
            cp.wait_send()


GATHER_SEMS = [pltpu.SemaphoreType.DMA((7,)), pltpu.SemaphoreType.DMA((7,)), pltpu.SemaphoreType.DMA]


class PlaneGather:
    def __init__(self, me, chunk, whole, y_first, send, recv, local):
        y, z = me.y, me.z
        first, second = (me.along_y, me.along_z) if y_first else (me.along_z, me.along_y)
        self.own = pltpu.make_async_copy(chunk, whole.at[:, y, z], local)
        self.one = [
            remote(chunk, whole.at[:, y, z], send.at[k - 1], recv.at[k - 1], first(k)) for k in (1, 3, 2)
        ]
        line = whole.at[:, :, z] if y_first else whole.at[:, y]
        self.two = [remote(line, line, send.at[k + 2], recv.at[k + 2], second(k)) for k in (1, 3, 2)]

    def start(self):
        self.own.start()
        for cp in self.one:
            cp.start()

    def middle(self):
        self.own.wait()
        for cp in self.one:
            cp.wait_recv()
        for cp in self.two:
            cp.start()

    def finish(self):
        for cp in self.two:
            cp.wait_recv()
        for cp in self.one + self.two:
            cp.wait_send()


PLANE_SEMS = [pltpu.SemaphoreType.DMA((6,)), pltpu.SemaphoreType.DMA((6,)), pltpu.SemaphoreType.DMA]


class GroupReduce:
    def __init__(self, me, parts, sib, acc, blocks, send, recv):
        self.me, self.parts, self.sib, self.acc, self.blocks = me, parts, sib, acc, blocks
        self.cross, self.along = {}, {}
        for k in range(4):
            q = me.on(k) * 2 + 1 - me.c
            self.cross[k] = remote(parts.at[q], sib.at[k], send.at[k], recv.at[k], me.sibling())
            if k:
                self.along[k] = remote(acc.at[k], blocks.at[k], send.at[3 + k], recv.at[3 + k], me.ring(k))

    def over(self, k):
        self.cross[k].start()

    def ring(self, k):
        self.cross[k].wait_recv()
        total = self.parts[self.me.on(k) * 2 + self.me.c].astype(F32) + self.sib[k].astype(F32)
        if k:
            self.acc[k] = total.astype(BF)
            self.along[k].start()
        else:
            self.blocks[0] = total.astype(BF)

    def finish(self):
        for cp in self.along.values():
            cp.wait_recv()
        for cp in list(self.cross.values()) + list(self.along.values()):
            cp.wait_send()


REDUCE_SEMS = [pltpu.SemaphoreType.DMA((7,)), pltpu.SemaphoreType.DMA((7,))]


class PlaneReduce:
    def __init__(self, me, whole, cols, z_first, got1, part, got2, send, recv, total):
        self.me, self.z_first = me, z_first
        lo, n = cols
        self.view = lambda y, z: whole[:, y, z, :, lo : lo + n]
        self.got1, self.part, self.got2, self.total, self.cols = got1, part, got2, total, cols
        self.one, self.two = [], []
        for k in (1, 3, 2):
            if z_first:
                src, peer = whole.at[:, :, (me.z + k) % 4, :, lo : lo + n], me.along_z(k)
            else:
                src, peer = whole.at[:, (me.y + k) % 4, :, :, lo : lo + n], me.along_y(k)
            self.one.append(remote(src, got1.at[k - 1], send.at[k - 1], recv.at[k - 1], peer))
            to, peer = ((me.y + k) % 4, me.along_y(k)) if z_first else ((me.z + k) % 4, me.along_z(k))
            self.two.append(remote(part.at[to], got2.at[k - 1], send.at[k + 2], recv.at[k + 2], peer))

    def start(self):
        for cp in self.one:
            cp.start()

    def middle(self):
        me = self.me
        for cp in self.one:
            cp.wait_recv()

        def add(i, carry):
            mine = self.view(i, me.z) if self.z_first else self.view(me.y, i)
            s = mine.astype(F32)
            for k in range(3):
                s = s + self.got1[k, :, i].astype(F32)
            self.part[i] = s.astype(BF)
            return carry

        lax.fori_loop(0, 4, add, 0)
        for cp in self.two:
            cp.start()

    def finish(self):
        for cp in self.two:
            cp.wait_recv()
        lo, n = self.cols
        s = self.part[self.me.y if self.z_first else self.me.z].astype(F32)
        for k in range(3):
            s = s + self.got2[k].astype(F32)
        self.total[:, :, lo : lo + n] = s
        for cp in self.one + self.two:
            cp.wait_send()


def plane_reduce_scratch(n):
    return [
        pltpu.VMEM((3, 4, 4, 16, n), BF),
        pltpu.VMEM((4, 4, 16, n), BF),
        pltpu.VMEM((3, 4, 16, n), BF),
        pltpu.SemaphoreType.DMA((6,)),
        pltpu.SemaphoreType.DMA((6,)),
    ]


def row_exchange(me, total, got, send, recv, local):
    def rows(q):
        x, c = q // 2, q % 2
        return total.at[(x // 2) * 2 + c, pl.ds(pl.multiple_of((x % 2) * 8, 8), 8)]

    own = pltpu.make_async_copy(rows(me.p), got.at[me.p], local)
    out = []
    for k in range(1, 8):
        q, peer = me.group(k)
        out.append(remote(rows(q), got.at[me.p], send.at[k - 1], recv.at[k - 1], peer))
    return own, out


EXCHANGE_SEMS = [pltpu.SemaphoreType.DMA((7,)), pltpu.SemaphoreType.DMA((7,)), pltpu.SemaphoreType.DMA]


def start_all(cps):
    for cp in cps:
        cp.start()


def wait_all(cps):
    for cp in cps:
        cp.wait()


def iota(shape, dim):
    return lax.broadcasted_iota(jnp.int32, shape, dim)


def same_head():
    return (iota((128, 128), 0) < 64) == (iota((128, 128), 1) < 64)


def split(v):
    hi = v.astype(BF)
    return hi, (v - hi.astype(F32)).astype(BF)


def averager():
    j = jnp.where(same_head(), 1.0 / 64, 0.0).astype(BF)
    return jnp.concatenate([j, j], 0)


def means(v, avg):
    return dot(jnp.concatenate(split(v), 1), avg, NN)


def stack(v):
    v = v.astype(F32)
    first = iota(v.shape, 1) < 64
    return jnp.concatenate([jnp.where(first, v, 0.0), jnp.where(first, 0.0, v)], 0).astype(BF)


def fine(a, b, dims=NN):
    ah, al = split(a)
    bh, bl = split(b)
    return dot(ah, bh, dims) + dot(al, bh, dims) + dot(ah, bl, dims)


def masks():
    row, col = iota((128, 256), 0), iota((128, 256), 1) % 128
    br, bc = row // 16, col // 16
    earlier = jnp.where(bc < br, 1.0 / 16, 0.0)
    later = jnp.where(bc > br, 1.0 / 16, 0.0)
    low = earlier + jnp.where((bc == br) & (col <= row), 1.0 / (row % 16 + 1).astype(F32), 0.0)
    up = later + jnp.where((bc == br) & (row <= col), 1.0 / (col % 16 + 1).astype(F32), 0.0)
    return earlier, later, low, up


def head_params(wa_ref, p):
    mine = wa_ref[pl.ds(pl.multiple_of(p * 128, 128), 128), FB:].astype(F32)
    rows = mine.T
    both = jnp.where(iota((128, 128), 1) < 64, mine, pltpu.roll(mine, 64, 1))
    w0 = jnp.where(same_head(), both, 0.0)
    return w0, rows[INITB : INITB + 1], rows[IGAIN : IGAIN + 1], rows[IBIAS : IBIAS + 1]


def keep_rows(wa_ref, f, b):
    x, c = b // 2, b % 2
    rows = wa_ref[pl.ds(pl.multiple_of(((x // 2) * 2 + c) * 256 + f * 16, 16), 16), FB:].astype(F32)
    row = rows[(x % 2) * 8 : (x % 2) * 8 + 1]
    length = jnp.sum(jnp.where(iota((1, 128), 1) == LEN, row, 0.0), 1, keepdims=True)
    return jnp.where(iota((128, 128), 0).astype(F32) < length, 1.0, 0.0)


def rate_of(proj_ref, p):
    col = iota((128, 128), 1)
    pick = jnp.where(iota((128, 128), 0) == LR + 2 * p + jnp.where(col < 64, 0, 1), 1.0, 0.0).astype(BF)
    logits = dot(jnp.concatenate(split(proj_ref[:, FB:]), 1), jnp.concatenate([pick, pick], 0), NN)
    return (1.0 / 64) * jax.nn.sigmoid(logits)


def step_rows(ref, t):
    return jnp.concatenate([ref[b * 128 + t * 16 : b * 128 + t * 16 + 16] for b in range(8)], 0)


def rms(v):
    return lax.rsqrt(jnp.mean(v * v, -1, keepdims=True) + EPS)


def rms_back(v, gain, dy):
    r = rms(v)
    n = v * r
    inner = dy * gain
    return r * (inner - n * jnp.mean(inner * n, -1, keepdims=True)), jnp.sum(dy * n, 0, keepdims=True)


def fore_kernel(r):
    me = Place()
    greet(group_peers(me) + plane_peers(me))

    low = r.small[...].astype(F32)

    def put(buf, q, at, top, bottom):
        buf[q, :, at : at + top.shape[1]] = jnp.concatenate([top, bottom], 0).astype(BF)

    def cols(ref, at, n):
        return ref[:, at : at + n].astype(F32)

    for q in range(8):
        put(r.a_out, q, 0, cols(r.w_qkv, 128 * q, 128), cols(r.w_qkv, 2048 + 128 * q, 128))
        put(r.a_out, q, 128, cols(r.w_qkv, 1024 + 128 * q, 128), low)
    a_sends, b_sends = [], []
    for k in range(1, 8):
        q, peer = me.group(k)
        a_sends.append(remote(r.a_out.at[q], r.a_in.at[me.p], r.a_send.at[k - 1], r.a_recv.at[k - 1], peer))
        b_sends.append(remote(r.b_out.at[q], r.b_in.at[me.p], r.b_send.at[k - 1], r.b_recv.at[k - 1], peer))
    start_all(a_sends)
    tok = GroupGather(me, r.tokens, r.tok_all, *r.tok_sems)
    dout = GroupGather(me, r.d_out, r.dout_all, *r.dout_sems)
    tok.start()

    for n, w in enumerate((r.w_gate, r.w_up, r.w_down)):
        r.pad[n, :, FF - FF % 128 :] = jnp.zeros((8, 8 * FB - (FF - FF % 128)), F32)
        r.pad[n, :, :FF] = w[...].astype(F32)
    for q in range(8):
        half = 512 * (q % 2)
        put(r.b_out, q, 0, cols(r.w_out, half, 256), cols(r.w_out, half + 256, 256))
        put(r.b_out, q, 256, r.pad[0, :, FB * q : FB * q + FB], r.pad[1, :, FB * q : FB * q + FB])
        tail = jnp.concatenate([r.pad[2, :, FB * q + 256 : FB * q + FB], jnp.zeros((8, 128), F32)], 1)
        put(r.b_out, q, 640, r.pad[2, :, FB * q : FB * q + 256], tail)
    start_all(b_sends)

    def pairs(buf, dp):
        p0 = (dp // 2) * 4 + dp % 2
        r0, r1 = buf[p0].astype(F32), buf[p0 + 2].astype(F32)

        def rows(lo, n, at):
            return jnp.concatenate([r0[at : at + 8, lo : lo + n], r1[at : at + 8, lo : lo + n]], 0).astype(BF)

        return (lambda lo, n: rows(lo, n, 0)), (lambda lo, n: rows(lo, n, 8))

    r.a_in[me.p] = r.a_out[me.p]
    for cp in a_sends:
        cp.wait_recv()
    for dp in range(4):
        top, bottom = pairs(r.a_in, dp)
        r.chunk_a[dp, :, :128] = top(0, 128)
        r.chunk_a[dp, :, 128:256] = top(128, 128)
        r.chunk_a[dp, :, 256:384] = bottom(0, 128)
        r.chunk_a[dp, :, 384:512] = bottom(128, 128)
    pa = PlaneGather(me, r.chunk_a, r.wa, True, *r.pa_sems)
    po = PlaneGather(me, r.chunk_o, r.wo, False, *r.po_sems)
    pa.start()
    r.b_in[me.p] = r.b_out[me.p]
    for cp in b_sends:
        cp.wait_recv()
    for dp in range(4):
        top, bottom = pairs(r.b_in, dp)
        r.chunk_o[dp, :, :256] = top(0, 256)
        r.chunk_o[dp, :, 256:512] = bottom(0, 256)
        r.chunk_f[dp, :, :FB] = top(256, FB)
        r.chunk_f[dp, :, FB : 2 * FB] = bottom(256, FB)
        r.chunk_f[dp, :, 2 * FB : 2 * FB + 256] = top(640, 256)
        r.chunk_f[dp, :, 2 * FB + 256 :] = bottom(640, 128)
    pa.middle()
    po.start()
    for k in (1, 3, 2):
        tok.take(k)
    pa.finish()
    po.middle()
    dout.start()

    wa = r.wa.reshape(D, 512)
    vecs = wa[:, FB:].astype(F32).T[ATTN : ATTN + 8]
    r.vecs[...] = vecs
    gain = vecs[:1]
    avg = averager()
    for k in (0, 1, 3, 2):
        tok.got(k)
        x = me.back(k)
        rows = r.tok_all[pl.ds(x * 2, 2)].reshape(256, D).astype(F32)
        at = pl.ds(pl.multiple_of(x * 256, 256), 256)
        r.normed[at] = (rows * rms(rows) * gain).astype(BF)
        r.proj[at] = dot(r.normed[at], wa[...], NN)

    f = me.y * 4 + me.z
    w0, b0, gamma, beta = head_params(wa, me.p)
    w0 = w0 - jnp.where(same_head(), means(w0, avg), 0.0)
    b0 = b0 - means(jnp.broadcast_to(b0, (8, 128)), avg)[:1]
    gamma2 = gamma * gamma
    earlier, _, low_mask, _ = masks()
    r.rt[...] = rate_of(r.proj, me.p)
    for b in range(8):
        r.kp[b * 128 : b * 128 + 128] = keep_rows(wa, f, b)

    def prepare(b, carry):
        at = pl.ds(pl.multiple_of(b * 128, 128), 128)
        q, k, v = r.proj[at, :128], r.proj[at, 128:256], r.proj[at, 256:384]
        k2 = stack(k)
        r.ma[b] = ((dot(k.astype(BF), k2, NT) + 1.0) * earlier).astype(BF)
        r.mb[b] = ((dot(q.astype(BF), k2, NT) + 1.0) * low_mask).astype(BF)
        r.zb[at] = fine(k, w0) + b0
        r.a[at] = fine(q, w0) + b0
        r.gt[at] = gamma * (beta - v + k)
        r.g2[b] = jnp.zeros((256, 128), BF)
        return carry

    lax.fori_loop(0, 8, prepare, 0)
    r.mgt[...] = means(r.gt[...], avg)
    dout.take(1)
    dout.take(3)

    for t in range(8):
        z = step_rows(r.zb, t)
        if t:
            z = z - jnp.concatenate([dot(r.ma[b, t * 16 : t * 16 + 16], r.g2[b], NN) for b in range(8)], 0)
        gtt, keep, rate = step_rows(r.gt, t), step_rows(r.kp, t), step_rows(r.rt, t)
        gz = gamma2 * z
        m = means(jnp.concatenate([z * z, gz, gz * z, gtt * z], 0), avg)
        s = lax.rsqrt(m[:128] + EPS)
        n = z * s
        mu = keep * (s * m[128:256] + step_rows(r.mgt, t))
        mun = keep * s * (s * m[256:384] + m[384:])
        h = keep * (gamma2 * n + gtt) - mu - n * mun
        g = stack(rate * s * h)
        for b in range(8):
            r.z[b * 128 + t * 16 : b * 128 + t * 16 + 16] = z[b * 16 : b * 16 + 16]
            r.g2[b, t * 16 : t * 16 + 16] = g[b * 16 : b * 16 + 16]
            r.g2[b, 128 + t * 16 : 144 + t * 16] = g[128 + b * 16 : 144 + b * 16]

    def answer(b, carry):
        at = pl.ds(pl.multiple_of(b * 128, 128), 128)
        a = r.a[at] - dot(r.mb[b], r.g2[b], NN)
        r.a[at] = a
        na = a * lax.rsqrt(means(a * a, avg) + EPS)
        r.mixed[b] = (r.proj[at, :128] + gamma * na + beta).astype(BF)
        return carry

    lax.fori_loop(0, 8, answer, 0)
    dout.take(2)
    tok.done()
    for k in range(4):
        dout.got(k)
    dout.done()
    po.finish()
    for cp in a_sends + b_sends:
        cp.wait_send()


def core_kernel(r):
    me = Place()
    greet(group_peers(me) + plane_peers(me))
    fa = PlaneGather(me, r.chunk_f.at[:, :, :640], r.wf.at[:, :, :, :, :640], True, *r.fa_sems)
    fb = PlaneGather(me, r.chunk_f.at[:, :, 640:], r.wf.at[:, :, :, :, 640:], False, *r.fb_sems)
    here = r.full.at[:, pl.ds(pl.multiple_of(me.p * 128, 128), 128)]
    own = pltpu.make_async_copy(r.mixed.at[me.p], here, r.turn_sems[2])
    turn = []
    for k in range(1, 8):
        q, peer = me.group(k)
        turn.append(remote(r.mixed.at[q], here, r.turn_sems[0].at[k - 1], r.turn_sems[1].at[k - 1], peer))
    start_all(turn)
    own.start()
    wo_own = pltpu.make_async_copy(r.wo_half, r.wo.at[me.c], r.wo_sems[2])
    wo_over = remote(r.wo_half, r.wo.at[me.c], r.wo_sems[0], r.wo_sems[1], me.sibling())
    wo_own.start()
    wo_over.start()
    fa.start()
    fb.start()
    for cp in turn:
        cp.wait_recv()
    own.wait()
    wo_own.wait()
    wo_over.wait_recv()

    m = r.full[...].astype(F32)
    r.posted[...] = (m * rms(m) * r.vecs[POST - ATTN : POST - ATTN + 1]).astype(BF)
    for h in range(2):
        at = slice(512 * h, 512 * h + 512)
        wo = r.wo.at[h].reshape(D, 512)
        r.middle[:, at] = r.tokens[:, at].astype(F32) + dot(r.posted[...], wo[...], NN)
    mid = r.middle[...]
    r.ffn_in[...] = (mid * rms(mid) * r.vecs[FFN - ATTN : FFN - ATTN + 1]).astype(BF)

    x = GroupGather(me, r.ffn_in, r.x_all, *r.x_sems)
    x.start()
    fa.middle()
    fb.middle()
    red = GroupReduce(me, r.dx, r.sib, r.acc, r.blocks, *r.red_sems)
    wf = r.wf.reshape(D, 3 * FB)
    wg, wu, wd = (slice(FB * n, FB * n + FB) for n in range(3))

    def rows(k):
        c = me.back(k)
        two = pl.ds(c * 2, 2)
        at = pl.ds(pl.multiple_of(c * 256, 256), 256)
        xi = r.x_all[two].reshape(256, D)
        gate = dot(xi, wf[:, wg], NN)
        upper = dot(xi, wf[:, wu], NN)
        sigma = jax.nn.sigmoid(gate)
        active = gate * sigma
        hid = (active * upper).astype(BF)
        r.hidden[at] = hid
        dh = dot(r.dout_all[two].reshape(256, D), wf[:, wd], NN)
        dg = (dh * upper * (sigma + active * (1.0 - sigma))).astype(BF)
        du = (dh * active).astype(BF)
        r.dgu[at, :FB] = dg
        r.dgu[at, FB:] = du
        r.dx[two] = (dot(dg, wf[:, wg], NT) + dot(du, wf[:, wu], NT)).astype(BF).reshape(2, T, D)
        red.over((4 - k) % 4)
        r.out[two] = dot(hid, wf[:, wd], NT).astype(BF).reshape(2, T, D)

    fa.finish()
    fb.finish()
    x.got(0)
    rows(0)
    x.take(1)
    x.take(3)
    red.ring(0)
    x.got(1)
    rows(1)
    red.ring(3)
    x.got(3)
    rows(3)
    red.ring(1)
    x.take(2)
    x.got(2)
    rows(2)
    red.ring(2)
    for i in range(4):
        at = slice(256 * i, 256 * i + 256)
        g = dot(r.x_all[:, :, at].reshape(8 * T, 256), r.dgu[...], TN).astype(BF)
        r.g_ff[i, :, :, :, : 2 * FB] = g.reshape(4, 4, 16, 2 * FB)
        g = dot(r.dout_all[:, :, at].reshape(8 * T, 256), r.hidden[...], TN).astype(BF)
        r.g_ff[i, :, :, :, 2 * FB :] = g.reshape(4, 4, 16, FB)
    ga = PlaneReduce(me, r.g_ff, (0, 640), True, *r.ga, total=r.tot_f)
    gb = PlaneReduce(me, r.g_ff, (640, 512), False, *r.gb, total=r.tot_f)
    ga.start()
    gb.start()
    x.done()
    red.finish()

    dn = (r.blocks[0].astype(F32) + r.blocks[1].astype(F32)) + (r.blocks[2].astype(F32) + r.blocks[3].astype(F32))
    dn, g_ffn = rms_back(r.middle[...], r.vecs[FFN - ATTN : FFN - ATTN + 1], dn)
    dm = r.dout_all[me.p].astype(F32) + dn
    r.d_middle[...] = dm
    r.dbr[...] = dm.astype(BF)
    d_posted = dot(r.dbr[:, :512], r.wo.at[0].reshape(D, 512)[...], NT)
    d_posted = d_posted + dot(r.dbr[:, 512:], r.wo.at[1].reshape(D, 512)[...], NT)
    dmix, g_post = rms_back(
        r.full[...].astype(F32), r.vecs[POST - ATTN : POST - ATTN + 1], d_posted
    )
    r.d_mixed[...] = dmix.astype(BF)
    own = pltpu.make_async_copy(
        r.d_mixed.at[:, pl.ds(pl.multiple_of(me.p * 128, 128), 128)], r.dmix.at[me.p], r.back_sems[2]
    )
    own.start()
    back = []
    for k in range(1, 8):
        q, peer = me.group(k)
        src = r.d_mixed.at[:, pl.ds(pl.multiple_of(q * 128, 128), 128)]
        back.append(remote(src, r.dmix.at[me.p], r.back_sems[0].at[k - 1], r.back_sems[1].at[k - 1], peer))
    start_all(back)
    r.vec[...] = jnp.concatenate([g_ffn, g_post, jnp.zeros((6, D), F32)], 0)
    ga.middle()
    gb.middle()
    for h in range(2):
        g = dot(r.posted[...], r.dbr[:, 512 * h : 512 * h + 512], TN).astype(BF)
        r.g_o[h] = g.reshape(4, 4, 4, 16, 512)
    wait_all(back)
    own.wait()
    for cp in turn + [wo_over]:
        cp.wait_send()
    ga.finish()
    gb.finish()


def aft_kernel(r):
    me = Place()
    greet(group_peers(me) + plane_peers(me))
    out = GroupReduce(me, r.out, r.out_sib, r.out_acc, r.out_blocks, *r.out_sems)
    for k in range(4):
        out.over(k)
    mine_f, rows_f = row_exchange(me, r.tot_f, r.got_f, *r.f_sems)
    mine_f.start()
    start_all(rows_f)
    o_over = remote(r.g_o.at[1 - me.c], r.o_sib, r.o_sems[0], r.o_sems[1], me.sibling())
    o_over.start()

    p, f = me.p, me.y * 4 + me.z
    avg = averager()
    wa = r.wa.reshape(D, 512)
    w0, _, gamma, beta = head_params(wa, p)
    w0 = w0 - jnp.where(same_head(), means(w0, avg), 0.0)
    gamma2 = gamma * gamma
    earlier, later, low, up = masks()
    r.rt[...] = rate_of(r.proj, p)
    for b in range(8):
        r.kp[b * 128 : b * 128 + 128] = keep_rows(wa, f, b)
    r.sums[...] = jnp.zeros((8, 128), F32)

    def prepare(b, carry):
        at = pl.ds(pl.multiple_of(b * 128, 128), 128)
        q, k, v = r.proj[at, :128], r.proj[at, 128:256], r.proj[at, 256:384]
        z, keep = r.z[at], r.kp[at]
        s = lax.rsqrt(means(z * z, avg) + EPS)
        n = z * s
        gn = gamma2 * n
        u = keep * (gn + gamma * (beta - v + k))
        m = means(jnp.concatenate([u, u * n, gn, gn * n], 0), avg)
        r.s[at], r.n[at], r.u[at] = s, n, u
        r.h[at] = u - m[:128] - n * m[128:256]
        r.mun[at], r.mg1[at], r.mg2[at] = m[128:256], m[256:384], m[384:]
        a = r.a[at]
        sa = lax.rsqrt(means(a * a, avg) + EPS)
        na = a * sa
        d = r.dmix[b].astype(F32)
        dna = d * gamma
        da = sa * (dna - na * means(dna * na, avg))
        r.da[at] = da
        r.sums[0:1] += jnp.sum(d * na, 0, keepdims=True)
        r.sums[1:2] += jnp.sum(d, 0, keepdims=True)
        kb = k.astype(BF)
        mbt = ((dot(kb, stack(q), NT) + 1.0) * up).astype(BF)
        r.dgb[at] = -dot(mbt, stack(da), NN)
        r.mat[b] = ((dot(kb, stack(k), NT) + 1.0) * later).astype(BF)
        r.dz2[b] = jnp.zeros((256, 128), BF)
        return carry

    lax.fori_loop(0, 8, prepare, 0)
    for k in (2, 1, 3, 0):
        out.ring(k)
    o_over.wait_recv()

    def add(i, carry):
        for j in range(4):
            r.o_sum[i, j] = (r.g_o[me.c, i, j].astype(F32) + r.o_sib[i, j].astype(F32)).astype(BF)
        return carry

    lax.fori_loop(0, 4, add, 0)
    go = PlaneReduce(me, r.o_sum, (0, 512), False, *r.go, total=r.tot_o)
    go.start()

    for t in range(7, -1, -1):
        g = step_rows(r.dgb, t)
        if t < 7:
            g = g - jnp.concatenate([dot(r.mat[b, t * 16 : t * 16 + 16], r.dz2[b], NN) for b in range(8)], 0)
        s, n, u, h = step_rows(r.s, t), step_rows(r.n, t), step_rows(r.u, t), step_rows(r.h, t)
        mun, keep = step_rows(r.mun, t), step_rows(r.kp, t)
        dh = s * step_rows(r.rt, t) * g
        dhn = dh * n
        m = means(jnp.concatenate([dh, dhn, dh * h, gamma2 * dhn], 0), avg)
        md, cc = m[:128], m[128:256]
        du = dh - md - cc * n
        mdn = keep * (m[384:] - md * step_rows(r.mg1, t) - cc * step_rows(r.mg2, t)) - 2.0 * mun * cc
        dn = keep * gamma2 * du - mun * dh - cc * u
        dz = s * (dn - n * (m[256:384] + mdn))
        dzs = stack(dz)
        for b in range(8):
            at, here = slice(b * 128 + t * 16, b * 128 + t * 16 + 16), slice(b * 16, b * 16 + 16)
            r.dz[at], r.du[at], r.dgp[at] = dz[here], du[here], g[here]
            r.dz2[b, t * 16 : t * 16 + 16] = dzs[here]
            r.dz2[b, 128 + t * 16 : 144 + t * 16] = dzs[128 + b * 16 : 144 + b * 16]
    go.middle()

    col, row = iota((128, 128), 1), iota((128, 128), 0)
    place = jnp.where(
        ((row == 0) & (col == LR + 2 * p)) | ((row == 64) & (col == LR + 2 * p + 1)), 1.0, 0.0
    ).astype(BF)

    def finish(b, carry):
        at = pl.ds(pl.multiple_of(b * 128, 128), 128)
        q, k, v = r.proj[at, :128], r.proj[at, 128:256], r.proj[at, 256:384]
        s, n, du, keep, rate = r.s[at], r.n[at], r.du[at], r.kp[at], r.rt[at]
        da, dz, g = r.da[at], r.dz[at], s * r.h[at]
        dt = keep * gamma * du
        r.sums[0:1] += jnp.sum(keep * (2.0 * gamma * n + (beta - v + k)) * du, 0, keepdims=True)
        r.sums[1:2] += jnp.sum(dt, 0, keepdims=True)
        r.sums[2:3] += jnp.sum(da + dz, 0, keepdims=True)
        drate = 64.0 * means(r.dgp[at] * g, avg)
        dl = drate * rate * (1.0 - 64.0 * rate)
        gr = rate * g
        gb, dab, dzb = gr.astype(BF), da.astype(BF), dz.astype(BF)
        g2, k2, da2 = stack(gr), stack(k), stack(da)
        sb = (dot(dab, g2, NT) * low).astype(BF)
        sbt = (dot(gb, da2, NT) * up).astype(BF)
        sa = (dot(dzb, g2, NT) * earlier + dot(gb, r.dz2[b], NT) * later).astype(BF)
        dq = r.dmix[b].astype(F32) + fine(da, w0, NT) - dot(sb, k2, NN)
        dk = dt + fine(dz, w0, NT) - dot(sbt, stack(q), NN) - dot(sa, k2, NN)
        r.dp[at, :128] = dq.astype(BF)
        r.dp[at, 128:256] = dk.astype(BF)
        r.dp[at, 256:384] = (-dt).astype(BF)
        r.dp[at, 384:] = dot(dl.astype(BF), place, NN).astype(BF)
        return carry

    lax.fori_loop(0, 8, finish, 0)
    dw = dot(r.proj[:, 128:256].astype(BF), r.dz[...].astype(BF), TN)
    dw = dw + dot(r.proj[:, :128].astype(BF), r.da[...].astype(BF), TN)
    dw = dw - means(dw, avg)
    dw = jnp.where(row < 64, dw, pltpu.roll(dw, 64, 1))
    dw = jnp.where(col < 64, dw, 0.0)
    sm = r.sums[...]
    db = sm[2:3] - means(jnp.broadcast_to(sm[2:3], (8, 128)), avg)[:1]
    mine = jnp.where(row == INITB, db, 0.0) + jnp.where(row == IGAIN, sm[0:1], 0.0)
    mine = mine + jnp.where(row == IBIAS, sm[1:2], 0.0)
    r.mine[...] = dw + mine.T

    big = iota((128, D), 0)
    vrows = jnp.where(big == FFN, r.vec[0:1], 0.0) + jnp.where(big == POST, r.vec[1:2], 0.0)
    vrows = vrows + jnp.where(big == ATTN, 1.0 / r.vecs[0:1], 0.0)
    where = iota((256, 128), 1)
    for i in range(4):
        at = slice(256 * i, 256 * i + 256)
        g = dot(r.normed[:, at], r.dp[...], TN)
        cols = vrows[:, at].T
        attn = jnp.sum(g * wa[at].astype(F32), 1, keepdims=True)
        cols = jnp.where(where == ATTN, cols * attn, cols)
        r.g_a[i, :, :, :, :FB] = g[:, :FB].astype(BF).reshape(4, 4, 16, FB)
        r.low[at] = (g[:, FB:] + cols).astype(BF)
    at = pl.ds(pl.multiple_of(p * 128, 128), 128)
    r.low[at] = (r.low[at].astype(F32) + r.mine[...]).astype(BF)
    r.g_a[:, :, :, :, FB:] = r.low[...].reshape(4, 4, 4, 16, 128)
    ga = PlaneReduce(me, r.g_a, (0, 512), True, *r.ga, total=r.tot_a)
    ga.start()
    red = GroupReduce(me, r.dn, r.sib, r.acc, r.blocks, *r.red_sems)
    order = (2, 1, 3, 0)
    for n, k in enumerate(order):
        c = me.on(k)
        at = pl.ds(pl.multiple_of(c * 256, 256), 256)
        r.dn[pl.ds(c * 2, 2)] = dot(r.dp[at], wa[...], NT).astype(BF).reshape(2, T, D)
        red.over(k)
        if n:
            red.ring(order[n - 1])
    red.ring(order[-1])
    go.finish()
    mine_o, rows_o = row_exchange(me, r.tot_o, r.got_o, *r.ox_sems)
    mine_o.start()
    start_all(rows_o)
    ga.middle()
    out.finish()
    wait_all(rows_f)
    mine_f.wait()
    o_over.wait_send()
    ga.finish()
    mine_a, rows_a = row_exchange(me, r.tot_a, r.got_a, *r.ax_sems)
    mine_a.start()
    start_all(rows_a)
    red.finish()
    wait_all(rows_o)
    mine_o.wait()
    wait_all(rows_a)
    mine_a.wait()


def end_kernel(r):
    def total(ref):
        return (ref[0].astype(F32) + ref[1].astype(F32)) + (ref[2].astype(F32) + ref[3].astype(F32))

    r.output[...] = (r.middle[...] + total(r.out_blocks)).astype(BF)
    d, _ = rms_back(r.tokens[...].astype(F32), r.vecs[0:1], total(r.blocks))
    r.d_tok[...] = r.d_middle[...] + d
    small = jnp.zeros((8, 128), F32)
    for q in range(8):
        for n in range(3):
            r.g_qkv[:, 1024 * n + 128 * q : 1024 * n + 128 * q + 128] = r.got_a[q, :, 128 * n : 128 * n + 128]
        small = small + r.got_a[q, :, FB:]
        w = min(FB, FF - FB * q)
        for n, ref in enumerate((r.g_gate, r.g_up, r.g_down)):
            ref[:, FB * q : FB * q + w] = r.got_f[q, :, FB * n : FB * n + w]
    r.g_small[...] = small
    for h in range(2):
        at = slice(512 * h, 512 * h + 512)
        r.g_out[:, at] = (r.got_o[h] + r.got_o[2 + h]) + (r.got_o[4 + h] + r.got_o[6 + h])


DMA = pltpu.SemaphoreType.DMA


def call(kernel, name, args, outs, scratch, collective=None, limit=60):
    flat, counts = [], []
    for shape in scratch.values():
        group = list(shape) if isinstance(shape, (list, tuple)) else [shape]
        counts.append((len(group), isinstance(shape, (list, tuple))))
        flat += group

    def body(*refs):
        given = dict(zip(list(args) + list(outs), refs))
        at = len(args) + len(outs)
        for key, (n, many) in zip(scratch, counts):
            given[key] = refs[at : at + n] if many else refs[at]
            at += n
        kernel(SimpleNamespace(**given))

    params = dict(vmem_limit_bytes=limit * 1024 * 1024)
    if collective is not None:
        params.update(collective_id=collective, has_side_effects=True)
    results = pl.pallas_call(
        body,
        name=name,
        out_shape=[jax.ShapeDtypeStruct(s, d) for s, d, _ in outs.values()],
        in_specs=[spec for _, spec in args.values()],
        out_specs=[spec for _, _, spec in outs.values()],
        scratch_shapes=flat,
        compiler_params=pltpu.CompilerParams(**params),
    )(*[a for a, _ in args.values()])
    return SimpleNamespace(**dict(zip(outs, results)))


def big(n, t):
    return pltpu.VMEM((8 * T, n), t)


def local(
    tokens, lengths, attn_gain, w_qkv, w_lr, init_w, init_b, inner_gain, inner_bias,
    post_gain, w_out, ffn_gain, w_gate, w_up, w_down, d_out,
):
    vectors = (attn_gain, init_b, inner_gain, inner_bias, post_gain, ffn_gain)
    length = jnp.broadcast_to(lengths.astype(BF).reshape(1, 1), (8, 1))
    small = jnp.concatenate(
        [init_w, w_lr] + [v.reshape(8, 1) for v in vectors] + [length, jnp.zeros((8, 41), BF)], 1
    )
    grid = lambda n: (4, 4, 4, 16, n)
    all8, four = (8, T, D), (4, T, D)
    s = call(
        fore_kernel,
        "fore",
        dict(
            w_qkv=(w_qkv, VMEM), small=(small, VMEM), w_out=(w_out, VMEM), w_gate=(w_gate, VMEM),
            w_up=(w_up, VMEM), w_down=(w_down.T, VMEM), tokens=(tokens, HBM), d_out=(d_out, HBM),
        ),
        dict(
            wa=(grid(512), BF, VMEM), wo=(grid(512), BF, HBM), chunk_f=((4, 16, 3 * FB), BF, VMEM),
            dout_all=(all8, BF, HBM), vecs=((8, D), F32, VMEM), normed=((8 * T, D), BF, VMEM),
            proj=((8 * T, 512), F32, VMEM), mixed=((8, T, 128), BF, VMEM), z=((8 * T, 128), F32, VMEM),
            a=((8 * T, 128), F32, VMEM),
        ),
        dict(
            pad=pltpu.VMEM((3, 8, 8 * FB), F32),
            a_out=pltpu.VMEM((8, 16, 256), BF), a_in=pltpu.VMEM((8, 16, 256), BF),
            b_out=pltpu.VMEM((8, 16, 896), BF), b_in=pltpu.VMEM((8, 16, 896), BF),
            chunk_a=pltpu.VMEM((4, 16, 512), BF), chunk_o=pltpu.VMEM((4, 16, 512), BF),
            tok_all=pltpu.VMEM(all8, BF),
            a_send=DMA((7,)), a_recv=DMA((7,)), b_send=DMA((7,)), b_recv=DMA((7,)),
            tok_sems=GATHER_SEMS, dout_sems=GATHER_SEMS, pa_sems=PLANE_SEMS, po_sems=PLANE_SEMS,
            ma=pltpu.VMEM((8, 128, 256), BF), mb=pltpu.VMEM((8, 128, 256), BF),
            zb=big(128, F32), gt=big(128, F32), mgt=big(128, F32), kp=big(128, F32), rt=big(128, F32),
            g2=pltpu.VMEM((8, 256, 128), BF),
        ),
        collective=1,
    )
    m = call(
        core_kernel,
        "core",
        dict(
            mixed=(s.mixed, VMEM), tokens=(tokens, VMEM), wo_half=(s.wo, HBM), vecs=(s.vecs, VMEM),
            chunk_f=(s.chunk_f, VMEM), dout_all=(s.dout_all, VMEM),
        ),
        dict(
            middle=((T, D), F32, VMEM), d_middle=((T, D), F32, VMEM), dmix=((8, T, 128), BF, VMEM),
            g_o=((2,) + grid(512), BF, VMEM), vec=((8, D), F32, VMEM), out=(all8, BF, VMEM),
            tot_f=((4, 16, 3 * FB), F32, VMEM),
        ),
        dict(
            full=pltpu.VMEM((T, D), BF), posted=pltpu.VMEM((T, D), BF), ffn_in=pltpu.VMEM((T, D), BF),
            dbr=pltpu.VMEM((T, D), BF), d_mixed=pltpu.VMEM((T, D), BF), x_all=pltpu.VMEM(all8, BF),
            wf=pltpu.VMEM(grid(3 * FB), BF), wo=pltpu.VMEM((2,) + grid(512), BF),
            hidden=big(FB, BF), dgu=big(2 * FB, BF), dx=pltpu.VMEM(all8, BF),
            sib=pltpu.VMEM(four, BF), acc=pltpu.VMEM(four, BF), blocks=pltpu.VMEM(four, BF),
            g_ff=pltpu.VMEM(grid(3 * FB), BF),
            fa_sems=PLANE_SEMS, fb_sems=PLANE_SEMS, turn_sems=EXCHANGE_SEMS, back_sems=EXCHANGE_SEMS,
            wo_sems=[DMA, DMA, DMA], x_sems=GATHER_SEMS, red_sems=REDUCE_SEMS,
            ga=plane_reduce_scratch(640), gb=plane_reduce_scratch(512),
        ),
        collective=2,
    )
    t = call(
        aft_kernel,
        "aft",
        dict(
            dmix=(m.dmix, VMEM), wa=(s.wa, VMEM), normed=(s.normed, VMEM), proj=(s.proj, VMEM),
            z=(s.z, VMEM), a=(s.a, VMEM), vec=(m.vec, VMEM), vecs=(s.vecs, VMEM), out=(m.out, VMEM),
            g_o=(m.g_o, VMEM), tot_f=(m.tot_f, VMEM),
        ),
        dict(
            blocks=(four, BF, VMEM), out_blocks=(four, BF, VMEM), got_a=((8, 8, 512), F32, VMEM),
            got_o=((8, 8, 512), F32, VMEM), got_f=((8, 8, 3 * FB), F32, VMEM),
        ),
        dict(
            **{n: big(128, F32) for n in ("rt", "kp", "s", "n", "u", "h", "mun", "mg1", "mg2", "da", "dgb")},
            **{n: big(128, F32) for n in ("dz", "du", "dgp")},
            mat=pltpu.VMEM((8, 128, 256), BF), dz2=pltpu.VMEM((8, 256, 128), BF), dp=big(512, BF),
            sums=pltpu.VMEM((8, 128), F32), mine=pltpu.VMEM((128, 128), F32), low=pltpu.VMEM((D, 128), BF),
            dn=pltpu.VMEM(all8, BF), g_a=pltpu.VMEM(grid(512), BF),
            sib=pltpu.VMEM(four, BF), acc=pltpu.VMEM(four, BF), out_sib=pltpu.VMEM(four, BF),
            out_acc=pltpu.VMEM(four, BF), o_sib=pltpu.VMEM(grid(512), BF), o_sum=pltpu.VMEM(grid(512), BF),
            tot_a=pltpu.VMEM((4, 16, 512), F32), tot_o=pltpu.VMEM((4, 16, 512), F32),
            out_sems=REDUCE_SEMS, red_sems=REDUCE_SEMS, o_sems=[DMA, DMA],
            f_sems=EXCHANGE_SEMS, ox_sems=EXCHANGE_SEMS, ax_sems=EXCHANGE_SEMS,
            ga=plane_reduce_scratch(512), go=plane_reduce_scratch(512),
        ),
        collective=3,
    )
    e = call(
        end_kernel,
        "end",
        dict(
            blocks=(t.blocks, VMEM), out_blocks=(t.out_blocks, VMEM), middle=(m.middle, VMEM),
            d_middle=(m.d_middle, VMEM), tokens=(tokens, VMEM), vecs=(s.vecs, VMEM), got_a=(t.got_a, VMEM),
            got_o=(t.got_o, VMEM), got_f=(t.got_f, VMEM),
        ),
        dict(
            output=((T, D), BF, VMEM), d_tok=((T, D), F32, VMEM), g_qkv=((8, 3 * D), F32, VMEM),
            g_small=((8, 128), F32, VMEM), g_out=((8, D), F32, VMEM), g_gate=((8, FF), F32, VMEM),
            g_up=((8, FF), F32, VMEM), g_down=((8, FF), F32, VMEM),
        ),
        {},
    )
    col = lambda n: e.g_small[:, n]
    return (
        e.output, e.d_tok, col(ATTN), e.g_qkv, e.g_small[:, LR:ATTN], e.g_small[:, :LR], col(INITB),
        col(IGAIN), col(IBIAS), col(POST), e.g_out, col(FFN), e.g_gate, e.g_up, e.g_down.T,
    )


def solution(mesh):
    both = ("dp", "fsdp")
    row, vec, down = P(both, None), P(both), P(None, both)
    return jax.shard_map(
        local,
        mesh=mesh,
        in_specs=(row, vec, vec, row, row, row, vec, vec, vec, vec, row, vec, row, row, down, row),
        out_specs=(row, row, vec, row, row, row, vec, vec, vec, vec, row, vec, row, row, down),
        check_vma=False,
    )
```
